512 devices in a mesh: ep: 128 (over y, z, core), tp: 4 (over x).
Axes of the slice: x: 4, y: 8, z: 8, core: 2. Of those that a mesh axis runs over, the one named last changes fastest.
Arguments:
- residual_in: bfloat16 [768, 2048], P('ep'), may hold values from -6 to 6
- new_query: bfloat16 [768, 2048], P('ep', 'tp'), may hold values from -6 to 6
- new_keys: bfloat16 [768, 2048], P('ep', 'tp'), may hold values from -6 to 6
- new_values: bfloat16 [768, 4096], P('ep', 'tp'), may hold values from -6 to 6
- out_gate: bfloat16 [768, 4096], P('ep', 'tp'), may hold values from -6 to 6
- beta_logit: float32 [768, 32], P('ep', 'tp'), may hold values from -6 to 6
- decay_logit: float32 [768, 32], P('ep', 'tp'), may hold values from -6 to 6
- decay_base: float32 [32], P('tp'), may hold values from -1 to 1.5
- decay_bias: float32 [32], P('tp'), may hold values from -2 to 1
- norm_gain: float32 [128], replicated, may hold values from 0.5 to 1.5
- state_store: bfloat16 [768, 32, 128, 128], P('ep', 'tp'), may hold values from -6 to 6
- state_scale: float32 [768, 32], P('ep', 'tp'), may hold values from 0.01 to 0.1
- arrival: int32 [768], P('ep'), may hold values from 0 to 5, as said below
- out_weight: bfloat16 [4096, 2048], P('tp', 'ep'), may hold values from -0.09375 to 0.09375
- ffn_gain: float32 [2048], replicated, may hold values from 0.5 to 1.5
- expert_gate_weight: bfloat16 [256, 2048, 512], P('ep', None, 'tp'), may hold values from -0.125 to 0.125
- expert_up_weight: bfloat16 [256, 2048, 512], P('ep', None, 'tp'), may hold values from -0.125 to 0.125
- expert_down_weight: bfloat16 [256, 512, 2048], P('ep', 'tp'), may hold values from -0.25 to 0.25
- route_ids: int32 [768, 10], P('ep'), may hold values from 0 to 255, as said below
- route_weight: float32 [768, 10], P('ep'), may hold values from 0.02 to 0.3
Outputs:
- mixed: bfloat16 [768, 2048], P('ep', 'tp')
The draws below stay inside these ranges and needn't reach their ends.
Inputs may be any that keep to these rules, and one draw needn't show every extreme that they name: `arrival`: each aligned block of 6 entries (the requests of one device) is a permutation of 0 to 5. `route_ids`: A row names 10 different experts. Within the rows of one device, an expert is named at most (315) // 256 times, and the experts e with the same e // 2 are named at most 1 times together; that bound is reached.
All inputs are finite; a program needn't handle non-finite values.
Results may differ from the reference program's by a relative error of at most 0.006.
Values may be sent and summed in bfloat16 or wider, within the bound.
A program may use at most 64 MiB of HBM per device.

```python
import math
import jax
import jax.numpy as jnp
from jax import lax

D = 2048
HV = 32
HK = 16
DK = 128
DV = 128
FFE = 512
TOP = 10
EXP_DEV = 2
REQ_DEV = 6
REQUESTS = 768
EXPERTS = 256


def draw_arrival(key, part):
    key = jax.random.fold_in(key, 5)
    block_keys = jax.random.split(key, REQUESTS // REQ_DEV)

    def block_order(block_key):
        return jax.random.permutation(block_key, REQ_DEV)
    return jax.vmap(block_order)(block_keys).reshape(REQUESTS).astype(jnp.int32)


def draw_route_ids(key, part):
    key = jax.random.fold_in(key, 11)
    hot_key, block_key = jax.random.split(key)
    owners = EXPERTS // EXP_DEV
    hot_owners = max(1, owners // 16)
    owner_rank = jax.random.permutation(hot_key, owners)
    hot_owner = (owner_rank < hot_owners).astype(jnp.int32)
    picks = REQ_DEV * TOP
    block_keys = jax.random.split(block_key, REQUESTS // REQ_DEV)

    def block_routes(one_key):
        noise_key, offset_key = jax.random.split(one_key)
        noise = jax.random.randint(noise_key, (owners,), 0, 1 << 20)
        score = (noise + hot_owner * (1 << 21)) * owners + jnp.arange(owners, dtype=jnp.int32)
        owner_order = jnp.argsort(-score).astype(jnp.int32)
        offsets = jax.random.randint(offset_key, (owners,), 0, EXP_DEV)
        rounds = jnp.arange(EXP_DEV, dtype=jnp.int32)[:, None]
        ranking = (owner_order[None, :] * EXP_DEV + (rounds + offsets[owner_order][None, :]) % EXP_DEV).reshape(EXPERTS)
        sequence = ranking[jnp.arange(picks) % EXPERTS]
        return sequence.reshape(REQ_DEV, TOP)
    return jax.vmap(block_routes)(block_keys).reshape(REQUESTS, TOP).astype(jnp.int32)


def level_of(own_key, extent, shards, smallest, top_value):
    gain = 1.0
    for axis_at, blocks in shards:
        draws = jax.random.uniform(jax.random.fold_in(jax.random.fold_in(own_key, 6), axis_at), (blocks,), jnp.float32, smallest / len(shards), top_value / len(shards))
        gain = gain * jnp.repeat(jnp.exp(draws), extent[axis_at] // blocks).reshape((-1,) + (1,) * (len(extent) - 1 - axis_at))
    return gain


def scatter_about(rng, shape, scale, most, pieces=(), kind=jnp.bfloat16):
    entries = scale * jax.random.normal(rng, shape, jnp.float32)
    if pieces:
        entries = entries * level_of(rng, shape, pieces, -0.22, 0.18)
    return jnp.clip(entries, -most, most).astype(kind)


def setup_inputs(seed: int = 0) -> dict:
    streams_of = jax.random.split(jax.random.key(seed), 21)
    residual_in = scatter_about(streams_of[0], (REQUESTS, D), 1.0, 6.0, ((0, 128),))
    new_query = scatter_about(streams_of[1], (REQUESTS, HK * DK), 1.0, 6.0, ((0, 128), (1, 4)))
    new_keys = scatter_about(streams_of[2], (REQUESTS, HK * DK), 1.0, 6.0, ((0, 128), (1, 4)))
    new_values = scatter_about(streams_of[3], (REQUESTS, HV * DV), 1.0, 6.0, ((0, 128), (1, 4)))
    out_gate = scatter_about(streams_of[4], (REQUESTS, HV * DV), 1.0, 6.0, ((0, 128), (1, 4)))
    beta_logit = scatter_about(streams_of[5], (REQUESTS, HV), 1.5, 6.0, ((0, 128), (1, 4)), jnp.float32)
    decay_logit = scatter_about(streams_of[6], (REQUESTS, HV), 1.0, 6.0, ((0, 128), (1, 4)), jnp.float32)
    decay_base = jnp.clip(-1.0 + 2.5 * jax.random.uniform(streams_of[7], (HV,), jnp.float32) ** level_of(streams_of[7], (HV,), ((0, 4),), -0.2, 0.2), -1.0, 1.5)
    decay_bias = jnp.clip(-2.0 + 3.0 * jax.random.uniform(streams_of[8], (HV,), jnp.float32) ** level_of(streams_of[8], (HV,), ((0, 4),), -0.2, 0.2), -2.0, 1.0)
    norm_gain = jnp.clip(1.0 + 0.1 * jax.random.normal(streams_of[9], (DV,), jnp.float32), 0.5, 1.5)
    state_store = scatter_about(streams_of[10], (REQUESTS, HV, DK, DV), 1.0, 6.0, ((0, 128), (1, 4)))
    state_scale = jnp.clip(jnp.exp(math.log(0.1) - 2.3025851 * jax.random.uniform(streams_of[11], (REQUESTS, HV), jnp.float32) ** level_of(streams_of[11], (REQUESTS, HV), ((0, 128), (1, 4)), -0.2, 0.2)), 0.01, 0.1)
    arrival = draw_arrival(jax.random.fold_in(streams_of[20], 71), 0)
    out_weight = scatter_about(streams_of[13], (HV * DV, D), (HV * DV) ** -0.5, 0.09375, ((0, 4), (1, 128)))
    ffn_gain = jnp.clip(1.0 + 0.1 * jax.random.normal(streams_of[14], (D,), jnp.float32), 0.5, 1.5)
    expert_gate_weight = scatter_about(streams_of[15], (EXPERTS, D, FFE), D ** -0.5, 0.125, ((0, 128), (2, 4)))
    expert_up_weight = scatter_about(streams_of[16], (EXPERTS, D, FFE), D ** -0.5, 0.125, ((0, 128), (2, 4)))
    expert_down_weight = scatter_about(streams_of[17], (EXPERTS, FFE, D), FFE ** -0.5, 0.25, ((0, 128), (1, 4)))
    route_ids = draw_route_ids(jax.random.fold_in(streams_of[20], 71), 0)
    route_weight = jnp.clip(jnp.exp(math.log(0.3) - 2.7080503 * jax.random.uniform(streams_of[19], (REQUESTS, TOP), jnp.float32) ** level_of(streams_of[19], (REQUESTS, TOP), ((0, 128),), -0.2, 0.2)), 0.02, 0.3)
    return {"residual_in": residual_in, "new_query": new_query, "new_keys": new_keys, "new_values": new_values, "out_gate": out_gate, "beta_logit": beta_logit, "decay_logit": decay_logit, "decay_base": decay_base, "decay_bias": decay_bias, "norm_gain": norm_gain, "state_store": state_store, "state_scale": state_scale, "arrival": arrival, "out_weight": out_weight, "ffn_gain": ffn_gain, "expert_gate_weight": expert_gate_weight, "expert_up_weight": expert_up_weight, "expert_down_weight": expert_down_weight, "route_ids": route_ids, "route_weight": route_weight}


def reference(residual_in, new_query, new_keys, new_values, out_gate, beta_logit, decay_logit, decay_base, decay_bias, norm_gain, state_store, state_scale, arrival, out_weight, ffn_gain, expert_gate_weight, expert_up_weight, expert_down_weight, route_ids, route_weight):
    group_size = HV // HK
    block_start = jnp.arange(REQUESTS, dtype=jnp.int32) // REQ_DEV * REQ_DEV
    state_rows = (block_start + arrival).astype(jnp.int32)

    def one_request(index):
        source_row = state_rows[index]
        query_heads = new_query[index].astype(jnp.float32).reshape(HK, DK)
        query_heads = query_heads / jnp.sqrt(lax.optimization_barrier(jnp.sum(query_heads * query_heads, axis=1, keepdims=True)) + 1e-06) / math.sqrt(DK)
        key_heads = new_keys[index].astype(jnp.float32).reshape(HK, DK)
        key_heads = key_heads / jnp.sqrt(lax.optimization_barrier(jnp.sum(key_heads * key_heads, axis=1, keepdims=True)) + 1e-06)
        query_heads = jnp.repeat(query_heads, group_size, axis=0)
        key_heads = jnp.repeat(key_heads, group_size, axis=0)
        value_heads = new_values[index].astype(jnp.float32).reshape(HV, DV)
        beta = jax.nn.sigmoid(beta_logit[index])
        decay = jnp.exp(-jnp.exp(decay_base) * jax.nn.softplus(decay_logit[index] + decay_bias))
        state = state_store[source_row].astype(jnp.float32) * (state_scale[source_row] * decay)[:, None, None]
        recalled = lax.optimization_barrier(jnp.sum(key_heads[:, :, None] * state, axis=1))
        delta = beta[:, None] * (value_heads - recalled)
        state = state + key_heads[:, :, None] * delta[:, None, :]
        heads = lax.optimization_barrier(jnp.sum(query_heads[:, :, None] * state, axis=1))
        gate_heads = out_gate[index].astype(jnp.float32).reshape(HV, DV)
        normed_heads = heads / jnp.sqrt(lax.optimization_barrier(jnp.mean(heads * heads, axis=1, keepdims=True)) + 1e-06) * norm_gain * jax.nn.silu(gate_heads)
        return normed_heads.reshape(HV * DV).astype(jnp.bfloat16)
    gated = lax.map(one_request, jnp.arange(REQUESTS, dtype=jnp.int32))
    attn = jnp.dot(gated, out_weight, preferred_element_type=jnp.float32).astype(jnp.bfloat16)
    carried = (residual_in.astype(jnp.float32) + attn.astype(jnp.float32)).astype(jnp.bfloat16)
    carried_wide = carried.astype(jnp.float32)
    normed = (carried_wide / jnp.sqrt(lax.optimization_barrier(jnp.mean(carried_wide * carried_wide, axis=1, keepdims=True)) + 1e-06) * ffn_gain).astype(jnp.bfloat16)
    per_expert = (REQ_DEV * TOP + EXPERTS - 1) // EXPERTS
    rows_most = REQUESTS // REQ_DEV * min(per_expert, REQ_DEV)

    def expert_step(total, expert):
        chosen = route_ids == expert
        weight_row = lax.optimization_barrier(jnp.sum(jnp.where(chosen, route_weight, 0.0), axis=1))
        picked_any = jnp.any(chosen, axis=1)
        row_index = jnp.nonzero(picked_any, size=rows_most, fill_value=0)[0].astype(jnp.int32)
        valid = (jnp.arange(rows_most) < jnp.sum(picked_any.astype(jnp.int32))).astype(jnp.float32)
        picked = normed[row_index]
        gate_projected = jnp.dot(picked, expert_gate_weight[expert], preferred_element_type=jnp.float32)
        up_projected = jnp.dot(picked, expert_up_weight[expert], preferred_element_type=jnp.float32)
        hidden_activation = (jax.nn.silu(gate_projected) * up_projected).astype(jnp.bfloat16)
        output_rows = jnp.dot(hidden_activation, expert_down_weight[expert], preferred_element_type=jnp.float32).astype(jnp.bfloat16)
        output_rows = lax.optimization_barrier(output_rows).astype(jnp.float32)
        contrib = output_rows * (weight_row[row_index] * valid)[:, None]
        return (total.at[row_index].add(contrib), None)
    start_total = jnp.zeros((REQUESTS, D), jnp.float32)
    total, unused = lax.scan(expert_step, start_total, jnp.arange(EXPERTS, dtype=jnp.int32))
    return (carried_wide + total).astype(jnp.bfloat16)
```

```python
import functools
import math

import jax
import jax.numpy as jnp
from jax import lax
from jax.experimental import pallas as pl
from jax.experimental.pallas import tpu as pltpu
from jax.sharding import PartitionSpec as P

MESH = pl.DeviceIdType.MESH
F32 = jnp.float32
BF16 = jnp.bfloat16
LANES = 128
PAD = 8
SRC = 2
ROWS = SRC * PAD
NT = (((1,), (1,)), ((), ()))
EXACT = lax.Precision.HIGHEST


def mm(a, b, dims=(((1,), (0,)), ((), ())), precision=None):
    return lax.dot_general(a, b, dims, preferred_element_type=F32, precision=precision)


def iota(shape, axis):
    return lax.broadcasted_iota(jnp.int32, shape, axis)


def silu(v):
    return v * jax.nn.sigmoid(v)


def whole_wait(ref, sem):
    pltpu.make_async_copy(ref, ref, sem).wait()


def kernel(
    nx,
    ny,
    nzc,
    top,
    residual,
    query,
    keys,
    values,
    out_gate,
    beta_logit,
    decay_logit,
    decay_base,
    decay_bias,
    norm_gain,
    state_scale,
    arrival,
    out_weight,
    ffn_gain,
    route_ids,
    route_weight,
    state_hbm,
    gate_hbm,
    up_hbm,
    down_hbm,
    out,
    stage,
    small,
    state,
    w_in,
    w_down,
    w_out,
    r0_src,
    r0_in,
    r1_src,
    r1_in,
    g_src,
    g_in,
    p_src,
    p_in,
    c_src,
    c_in,
    n_scr,
    place,
    weigh,
    masks,
    m3_src,
    m3_in,
    x_src,
    x_in,
    y_own,
    y_src,
    y_in,
    m6_src,
    m6_in,
    m7_src,
    m7_in,
    load_sem,
    send_sem,
    recv_sem,
):
    count, width = residual.shape
    chunks = width // LANES
    y_chunks = chunks // ny
    x_chunks = chunks // nx
    key_heads = query.shape[1] // LANES
    heads = 2 * key_heads
    slots = nzc * SRC
    groups = nzc // 8
    flat = 16 * chunks

    ep = lax.axis_index("ep")
    my_x = lax.axis_index("tp")
    my_y = ep // nzc
    my_zc = lax.rem(ep, nzc)

    def at_y(y):
        return (y * nzc + my_zc, my_x)

    def at_zc(zc):
        return (my_y * nzc + zc, my_x)

    def at_x(x):
        return (ep, x)

    ys = [lax.rem(my_y + d, ny) for d in range(1, ny)]
    zcs = [lax.rem(my_zc + d, nzc) for d in range(1, nzc)]
    xs = [lax.rem(my_x + d, nx) for d in range(1, nx)]

    sent = []

    def send(src, dst, hop, target):
        copy = pltpu.make_async_remote_copy(
            src_ref=src,
            dst_ref=dst,
            send_sem=send_sem.at[hop],
            recv_sem=recv_sem.at[hop],
            device_id=target,
            device_id_type=MESH,
        )
        copy.start()
        sent.append(copy)

    loads = [pltpu.make_async_copy(state_hbm, state, load_sem.at[0])]
    for e in range(2):
        span = pl.ds(e * LANES, LANES)
        loads.append(
            pltpu.make_async_copy(gate_hbm.at[e], w_in.at[:, pl.ds(e * LANES, LANES)], load_sem.at[1 + e])
        )
        loads.append(
            pltpu.make_async_copy(
                up_hbm.at[e], w_in.at[:, pl.ds((2 + e) * LANES, LANES)], load_sem.at[3 + e]
            )
        )
        loads.append(pltpu.make_async_copy(down_hbm.at[e], w_down.at[span, :], load_sem.at[5 + e]))
    for load in loads:
        load.start()

    barrier = pltpu.get_barrier_semaphore()
    greeted = 0
    for zc in zcs:
        pl.semaphore_signal(barrier, inc=1, device_id=at_zc(zc), device_id_type=MESH)
        greeted += 1
    for dx in range(nx):
        for dy in range(ny):
            if dx or dy:
                peer = (lax.rem(my_y + dy, ny) * nzc + my_zc, lax.rem(my_x + dx, nx))
                pl.semaphore_signal(barrier, inc=1, device_id=peer, device_id_type=MESH)
                greeted += 1

    stage[...] = jnp.zeros_like(stage)
    small[...] = jnp.zeros_like(small)
    q_at, k_at, v_at, g_at = 0, key_heads, 2 * key_heads, 2 * key_heads + heads
    r_at = g_at + heads
    for at, ref in ((q_at, query), (k_at, keys), (v_at, values), (g_at, out_gate), (r_at, residual)):
        stage[0:count, at * LANES : at * LANES + ref.shape[1]] = ref[...].astype(F32)

    small[0, 0:count, 0:top] = (route_ids[...] + 1).astype(F32)
    small[1, 0:count, 0:top] = route_weight[...]
    shift = my_y * top
    rolled_ids = pltpu.roll(small[0], shift, 1)
    rolled_weights = pltpu.roll(small[1], shift, 1)
    for y in range(ny):
        r0_src[y, 0:PAD, :] = rolled_ids
        r0_src[y, PAD : 2 * PAD, :] = rolled_weights
        for i in range(y_chunks):
            at = r_at + y * y_chunks + i
            r0_src[y, (2 + i) * PAD : (3 + i) * PAD, :] = stage[:, at * LANES : (at + 1) * LANES]

    own_cols = pl.ds(pl.multiple_of(my_zc * 16, 16), 16)
    eye = (iota((16, 16), 0) == iota((16, 16), 1)).astype(BF16)
    w_out[own_cols, :] = mm(eye, out_weight[...], NT).astype(BF16)
    r0_in[my_y] = r0_src[my_y]

    pl.semaphore_wait(barrier, greeted)

    for y in ys:
        send(r0_src.at[y], r0_in.at[my_y], 0, at_y(y))
    for zc in zcs:
        send(w_out.at[own_cols, :], w_out.at[own_cols, :], 1, at_zc(zc))

    loads[0].wait()
    small[2, 0:count, 0:heads] = decay_logit[...]
    small[3, 0:count, 0:heads] = beta_logit[...]
    rate = jnp.exp(decay_base[...])
    logit = small[2, :, 0:heads] + decay_bias[...]
    soft = jnp.maximum(logit, 0.0) + jnp.log1p(jnp.exp(-jnp.abs(logit)))
    decay = jnp.exp(-rate * soft)
    beta = jax.nn.sigmoid(small[3, :, 0:heads])
    row8 = iota((PAD, 1), 0)
    moved = jnp.zeros((PAD, heads), F32)
    for r in range(count):
        moved = jnp.where(row8 == r, state_scale[pl.ds(arrival[r], 1), :], moved)
    carry = moved * decay
    gain = norm_gain[...]

    for g in range(key_heads):
        q = stage[:, (q_at + g) * LANES : (q_at + g + 1) * LANES]
        k = stage[:, (k_at + g) * LANES : (k_at + g + 1) * LANES]
        q = q * (lax.rsqrt(jnp.sum(q * q, axis=1, keepdims=True) + 1e-06) / math.sqrt(LANES))
        k = k * lax.rsqrt(jnp.sum(k * k, axis=1, keepdims=True) + 1e-06)
        qk = jnp.sum(q * k, axis=1, keepdims=True)
        k_hi = k.astype(BF16).astype(F32)
        q_hi = q.astype(BF16).astype(F32)
        lhs = jnp.concatenate([k_hi, k - k_hi, q_hi, q - q_hi], axis=0).astype(BF16)
        from_k = jnp.zeros((PAD, 2 * LANES), F32)
        from_q = jnp.zeros((PAD, 2 * LANES), F32)
        for r in range(count):
            row = arrival[r]
            both = jnp.concatenate([state[row, 2 * g], state[row, 2 * g + 1]], axis=1)
            got = mm(lhs, both)
            from_k = jnp.where(row8 == r, got[0:8] + got[8:16], from_k)
            from_q = jnp.where(row8 == r, got[16:24] + got[24:32], from_q)
        pair = []
        for i in range(2):
            h = 2 * g + i
            s = carry[:, h : h + 1]
            v = stage[:, (v_at + h) * LANES : (v_at + h + 1) * LANES]
            z = stage[:, (g_at + h) * LANES : (g_at + h + 1) * LANES]
            delta = beta[:, h : h + 1] * (v - s * from_k[:, i * LANES : (i + 1) * LANES])
            o = s * from_q[:, i * LANES : (i + 1) * LANES] + qk * delta
            norm = lax.rsqrt(jnp.mean(o * o, axis=1, keepdims=True) + 1e-06)
            pair.append(o * norm * gain * silu(z))
        g_src[g * 16 : (g + 1) * 16, :] = jnp.concatenate(pair, axis=0).astype(BF16)

    for y in ys:
        send(g_src, g_in.at[my_y], 2, at_y(y))
    g_in[my_y] = g_src[...]

    whole_wait(r0_in.at[pl.ds(0, ny - 1)], recv_sem.at[0])
    ids = jnp.sum(r0_in[:, 0:PAD, :], axis=0)
    picks_w = jnp.sum(r0_in[:, PAD : 2 * PAD, :], axis=0)
    r1_src[...] = ids
    for zc in zcs:
        send(r1_src, r1_in.at[my_zc], 3, at_zc(zc))
    r1_in[my_zc] = ids

    sel_row = iota((32, LANES), 0)
    pick = jnp.bitwise_and(sel_row, 15)
    source = jnp.right_shift(sel_row, 4)
    sel = jnp.where(
        (iota((32, LANES), 1) == (SRC * my_x + source) * top + pick) & (pick < top), 1.0, 0.0
    ).astype(F32)
    spread = (iota((PAD, flat), 0) == jnp.bitwise_and(iota((PAD, flat), 1), 7)).astype(F32)
    flat_src = jnp.bitwise_and(jnp.right_shift(iota((16, flat), 1), 3), 1)

    def table(t):
        wide = mm(mm(sel, t, NT, EXACT), spread, precision=EXACT)
        return jnp.where(flat_src == 0, wide[0:16], wide[16:32])

    owner = jnp.floor((table(ids) - 1.0) * 0.5).astype(jnp.int32) - my_y * nzc
    weight = table(picks_w)
    zc_row = iota((nzc, flat), 0)
    hit = jnp.zeros((nzc, flat), F32)
    hit_w = jnp.zeros((nzc, flat), F32)
    for j in range(top):
        same = zc_row == owner[j : j + 1, :]
        hit = hit + jnp.where(same, 1.0, 0.0)
        hit_w = hit_w + jnp.where(same, weight[j : j + 1, :], 0.0)
    msg = SRC * chunks
    msg_row = iota((msg, flat), 0)
    msg_col = iota((msg, flat), 1)
    match = (
        jnp.bitwise_and(msg_row, chunks - 1) == jnp.right_shift(msg_col, 4)
    ) & (msg_row // chunks == jnp.bitwise_and(jnp.right_shift(msg_col, 3), 1))
    match = match.astype(F32)
    for zc in range(nzc):
        place[zc * msg : (zc + 1) * msg, :] = (hit[zc : zc + 1, :] * match).astype(BF16)
    weigh_t = hit_w.T
    hi = weigh_t.astype(BF16)
    lo = (weigh_t - hi.astype(F32)).astype(BF16)
    back = nzc * msg
    open_up = (iota((nzc, back), 0) == iota((nzc, back), 1) // msg).astype(BF16)
    w_row = iota((flat, back), 0)
    w_col = iota((flat, back), 1)
    kept = (jnp.right_shift(w_row, 4) == jnp.bitwise_and(w_col, chunks - 1)) & (
        jnp.bitwise_and(jnp.right_shift(w_row, 3), 1)
        == jnp.bitwise_and(w_col, msg - 1) // chunks
    )
    weigh[0] = jnp.where(kept, mm(hi, open_up), 0.0).astype(BF16)
    weigh[1] = jnp.where(kept, mm(lo, open_up), 0.0).astype(BF16)

    whole_wait(w_out.at[pl.ds(0, (nzc - 1) * 16), :], recv_sem.at[1])
    whole_wait(g_in.at[pl.ds(0, ny - 1)], recv_sem.at[2])
    first = jnp.zeros((ny * 16, nzc * 16), F32)
    second = jnp.zeros((ny * 16, nzc * 16), F32)
    for g in range(key_heads):
        rows = g_in[:, g * 16 : (g + 1) * 16, :].reshape(ny * 16, LANES)
        first += mm(rows, w_out[:, 2 * g * LANES : (2 * g + 1) * LANES], NT)
        second += mm(rows, w_out[:, (2 * g + 1) * LANES : (2 * g + 2) * LANES], NT)
    cols = nzc * 16
    part = first.reshape(ny, 2, PAD, cols)[:, 0] + second.reshape(ny, 2, PAD, cols)[:, 1]
    p_src[...] = part.reshape(nx, ROWS, cols)
    for x in xs:
        send(p_src.at[x], p_in.at[my_x], 4, at_x(x))
    p_in[my_x] = p_src[my_x]

    whole_wait(r1_in.at[pl.ds(0, nzc - 1)], recv_sem.at[3])
    slot = iota((nx * slots, nzc), 0)
    of_zc = jnp.right_shift(jnp.bitwise_and(slot, slots - 1), 1) == iota((nx * slots, nzc), 1)
    of_zc = of_zc.astype(BF16)
    slot = iota((nx * slots, LANES), 0)
    slot_y = SRC * (slot // slots) + jnp.bitwise_and(slot, 1)
    lane = iota((nx * slots, LANES), 1)
    of_y = (lane >= slot_y * top) & (lane < slot_y * top + top)
    arrived = r1_in[...]
    for e in range(2):
        named = (2 * ep + 1 + e).astype(F32)
        found = jnp.sum(jnp.where(arrived == named, 1.0, 0.0), axis=1).astype(BF16)
        found = jnp.where(of_y, mm(of_zc, found), 0.0)
        masks[e] = jnp.broadcast_to(jnp.sum(found, axis=1, keepdims=True), (nx * slots, LANES))

    whole_wait(p_in.at[pl.ds(0, nx - 1)], recv_sem.at[4])
    attn = p_in[0]
    for x in range(1, nx):
        attn = attn + p_in[x]
    attn = attn.astype(BF16).astype(F32)
    for i in range(y_chunks):
        base = jnp.concatenate(
            [r0_in[SRC * my_x + s, (2 + i) * PAD : (3 + i) * PAD, :] for s in range(SRC)], axis=0
        )
        c_src[i] = (base + attn[:, i * LANES : (i + 1) * LANES]).astype(BF16)
    for y in ys:
        send(c_src, c_in.at[my_y], 5, at_y(y))
    c_in[my_y] = c_src[...]
    whole_wait(c_in.at[pl.ds(0, ny - 1)], recv_sem.at[5])
    squares = jnp.zeros((ROWS, LANES), F32)
    for ch in range(chunks):
        c = c_in[ch // y_chunks, ch % y_chunks].astype(F32)
        squares = squares + c * c
    norm = lax.rsqrt(jnp.sum(squares, axis=1, keepdims=True) / width + 1e-06)
    for ch in range(chunks):
        c = c_in[ch // y_chunks, ch % y_chunks].astype(F32)
        n_scr[ch * 16 : (ch + 1) * 16, :] = (
            c * norm * ffn_gain[:, ch * LANES : (ch + 1) * LANES]
        ).astype(BF16)

    m3_src[...] = mm(place[...], n_scr[...]).astype(BF16).reshape(nzc, msg, LANES)
    for zc in zcs:
        send(m3_src.at[zc], m3_in.at[my_zc], 6, at_zc(zc))
    m3_in[my_zc] = m3_src[my_zc]
    turn_row = iota((flat, flat), 0)
    turn_col = iota((flat, flat), 1)
    unflat = (jnp.bitwise_and(turn_row, 15) == turn_col // chunks) & (
        jnp.right_shift(turn_row, 4) == jnp.bitwise_and(turn_col, chunks - 1)
    )
    unflat = unflat.astype(BF16)
    whole_wait(m3_in.at[pl.ds(0, nzc - 1)], recv_sem.at[6])
    for n in range(groups):
        block = mm(unflat, m3_in[n * 8 : (n + 1) * 8].reshape(flat, LANES)).astype(BF16)
        for ch in range(chunks):
            x_src[n * 16 : (n + 1) * 16, ch * LANES : (ch + 1) * LANES] = block[
                ch * 16 : (ch + 1) * 16
            ]
    for x in xs:
        send(x_src, x_in.at[my_x], 7, at_x(x))
    x_in[my_x] = x_src[...]

    for load in loads[1:]:
        load.wait()
    whole_wait(x_in.at[pl.ds(0, nx - 1)], recv_sem.at[7])
    rows = x_in[...].reshape(nx * slots, width)
    both = mm(rows, w_in[...])
    hidden = []
    for e in range(2):
        gate = both[:, e * LANES : (e + 1) * LANES]
        up = both[:, (2 + e) * LANES : (3 + e) * LANES]
        hidden.append(silu(gate) * up * masks[e])
    hidden = jnp.concatenate(hidden, axis=1).astype(BF16)
    result = mm(hidden, w_down[...]).reshape(nx, slots, width)
    y_own[...] = result
    y_src[...] = result.astype(BF16)
    for x in xs:
        send(y_src.at[x], y_in.at[my_x], 8, at_x(x))
    flatten = (jnp.bitwise_and(turn_col, 15) == turn_row // chunks) & (
        jnp.right_shift(turn_col, 4) == jnp.bitwise_and(turn_row, chunks - 1)
    )
    flatten = flatten.astype(BF16)
    y_in[my_x] = jnp.zeros_like(y_src[0])
    whole_wait(y_in.at[pl.ds(0, nx - 1)], recv_sem.at[8])

    for n in range(groups):
        tiles = []
        for ch in range(chunks):
            at = (pl.ds(n * 16, 16), pl.ds(ch * LANES, LANES))
            total = y_own[(my_x,) + at]
            for x in range(nx):
                total = total + y_in[(x,) + at].astype(F32)
            tiles.append(total.astype(BF16))
        block = mm(flatten, jnp.concatenate(tiles, axis=0)).astype(BF16)
        m6_src[n * 8 : (n + 1) * 8] = block.reshape(8, msg, LANES)
    for zc in zcs:
        send(m6_src.at[zc], m6_in.at[my_zc], 9, at_zc(zc))
    m6_in[my_zc] = m6_src[my_zc]
    whole_wait(m6_in.at[pl.ds(0, nzc - 1)], recv_sem.at[9])

    rows = m6_in[...].reshape(back, LANES)
    mixed = (mm(weigh[0], rows) + mm(weigh[1], rows)).reshape(chunks, ROWS, LANES)
    own_row = jnp.where(
        SRC * my_x + jnp.right_shift(iota((ROWS, LANES), 0), 3) == my_y, 1.0, 0.0
    ).astype(F32)
    for ch in range(chunks):
        c = c_in[ch // y_chunks, ch % y_chunks].astype(F32)
        m7_src[ch] = (mixed[ch] + c * own_row).reshape(SRC, PAD, LANES)
    for dx in range(nx):
        x = lax.rem(my_x + dx, nx)
        for s in range(SRC):
            y = SRC * my_x + s
            part = m7_src.at[pl.ds(x * x_chunks, x_chunks), s]
            if dx:
                send(part, m7_in.at[my_y], 10, (y * nzc + my_zc, x))
            else:
                keep = pltpu.make_async_copy(part, m7_in.at[my_y], recv_sem.at[10])
                away = pltpu.make_async_remote_copy(
                    src_ref=part,
                    dst_ref=m7_in.at[my_y],
                    send_sem=send_sem.at[10],
                    recv_sem=recv_sem.at[10],
                    device_id=(y * nzc + my_zc, x),
                    device_id_type=MESH,
                )

                @pl.when(y == my_y)
                def _():
                    keep.start()

                @pl.when(y != my_y)
                def _():
                    away.start()
                    away.wait_send()

    for copy in sent:
        copy.wait_send()
    whole_wait(m7_in, recv_sem.at[10])
    total = jnp.sum(m7_in[...], axis=0)
    for i in range(x_chunks):
        out[:, i * LANES : (i + 1) * LANES] = total[i, 0:count].astype(BF16)


def shards(
    nx,
    ny,
    nzc,
    residual_in,
    new_query,
    new_keys,
    new_values,
    out_gate,
    beta_logit,
    decay_logit,
    decay_base,
    decay_bias,
    norm_gain,
    state_store,
    state_scale,
    arrival,
    out_weight,
    ffn_gain,
    expert_gate_weight,
    expert_up_weight,
    expert_down_weight,
    route_ids,
    route_weight,
):
    count, width = residual_in.shape
    key_heads = new_query.shape[1] // LANES
    heads = 2 * key_heads
    top = route_ids.shape[1]
    chunks = width // LANES
    y_chunks = chunks // ny
    x_chunks = chunks // nx
    slots = nzc * SRC
    msg = SRC * chunks
    flat = 16 * chunks
    stage_tiles = 2 * key_heads + 2 * heads + chunks
    vmem = pl.BlockSpec(memory_space=pltpu.VMEM)
    smem = pl.BlockSpec(memory_space=pltpu.SMEM)
    anywhere = pl.BlockSpec(memory_space=pl.ANY)
    scratch = [
        pltpu.VMEM((PAD, stage_tiles * LANES), F32),
        pltpu.VMEM((4, PAD, LANES), F32),
        pltpu.VMEM(state_store.shape, BF16),
        pltpu.VMEM((width, 4 * LANES), BF16),
        pltpu.VMEM((2 * LANES, width), BF16),
        pltpu.VMEM((nzc * 16, heads * LANES), BF16),
        pltpu.VMEM((ny, (2 + y_chunks) * PAD, LANES), F32),
        pltpu.VMEM((ny, (2 + y_chunks) * PAD, LANES), F32),
        pltpu.VMEM((PAD, LANES), F32),
        pltpu.VMEM((nzc, PAD, LANES), F32),
        pltpu.VMEM((heads * PAD, LANES), BF16),
        pltpu.VMEM((ny, heads * PAD, LANES), BF16),
        pltpu.VMEM((nx, ROWS, nzc * 16), F32),
        pltpu.VMEM((nx, ROWS, nzc * 16), F32),
        pltpu.VMEM((y_chunks, ROWS, LANES), BF16),
        pltpu.VMEM((ny, y_chunks, ROWS, LANES), BF16),
        pltpu.VMEM((flat, LANES), BF16),
        pltpu.VMEM((nzc * msg, flat), BF16),
        pltpu.VMEM((2, flat, nzc * msg), BF16),
        pltpu.VMEM((2, nx * slots, LANES), F32),
        pltpu.VMEM((nzc, msg, LANES), BF16),
        pltpu.VMEM((nzc, msg, LANES), BF16),
        pltpu.VMEM((slots, width), BF16),
        pltpu.VMEM((nx, slots, width), BF16),
        pltpu.VMEM((nx, slots, width), F32),
        pltpu.VMEM((nx, slots, width), BF16),
        pltpu.VMEM((nx, slots, width), BF16),
        pltpu.VMEM((nzc, msg, LANES), BF16),
        pltpu.VMEM((nzc, msg, LANES), BF16),
        pltpu.VMEM((chunks, SRC, PAD, LANES), F32),
        pltpu.VMEM((ny, x_chunks, PAD, LANES), F32),
        pltpu.SemaphoreType.DMA((7,)),
        pltpu.SemaphoreType.DMA((11,)),
        pltpu.SemaphoreType.DMA((11,)),
    ]
    return pl.pallas_call(
        functools.partial(kernel, nx, ny, nzc, top),
        out_shape=jax.ShapeDtypeStruct((count, width // nx), BF16),
        in_specs=[vmem] * 11 + [smem] + [vmem] * 4 + [anywhere] * 4,
        out_specs=vmem,
        scratch_shapes=scratch,
        compiler_params=pltpu.CompilerParams(
            collective_id=0, has_side_effects=True, vmem_limit_bytes=40 * 1024 * 1024
        ),
        name="decode_layer",
    )(
        residual_in,
        new_query,
        new_keys,
        new_values,
        out_gate,
        beta_logit,
        decay_logit,
        decay_base[None, :],
        decay_bias[None, :],
        norm_gain[None, :],
        state_scale,
        arrival,
        out_weight,
        ffn_gain[None, :],
        route_ids,
        route_weight,
        state_store,
        expert_gate_weight,
        expert_up_weight,
        expert_down_weight,
    )


def solution(mesh):
    nx = mesh.shape["tp"]
    ny = SRC * nx
    nzc = mesh.shape["ep"] // ny
    return jax.shard_map(
        functools.partial(shards, nx, ny, nzc),
        mesh=mesh,
        in_specs=(
            P("ep", None),
            P("ep", "tp"),
            P("ep", "tp"),
            P("ep", "tp"),
            P("ep", "tp"),
            P("ep", "tp"),
            P("ep", "tp"),
            P("tp"),
            P("tp"),
            P(),
            P("ep", "tp", None, None),
            P("ep", "tp"),
            P("ep"),
            P("tp", "ep"),
            P(),
            P("ep", None, "tp"),
            P("ep", None, "tp"),
            P("ep", "tp", None),
            P("ep", None),
            P("ep", None),
        ),
        out_specs=P("ep", "tp"),
        check_vma=False,
    )
```

```python
import functools
import math

import jax
import jax.numpy as jnp
from jax import lax
from jax.experimental import pallas as pl
from jax.experimental.pallas import tpu as pltpu
from jax.sharding import PartitionSpec as P

MESH = pl.DeviceIdType.MESH
F32 = jnp.float32
BF16 = jnp.bfloat16
LANES = 128
PAD = 8
SRC = 2
ROWS = SRC * PAD
NT = (((1,), (1,)), ((), ()))
EXACT = lax.Precision.HIGHEST


def mm(a, b, dims=(((1,), (0,)), ((), ())), precision=None):
    return lax.dot_general(a, b, dims, preferred_element_type=F32, precision=precision)


def iota(shape, axis):
    return lax.broadcasted_iota(jnp.int32, shape, axis)


def silu(v):
    return v * jax.nn.sigmoid(v)


def whole_wait(ref, sem):
    pltpu.make_async_copy(ref, ref, sem).wait()


def kernel(
    nx,
    ny,
    nzc,
    top,
    residual_hbm,
    query_hbm,
    keys_hbm,
    values_hbm,
    out_gate_hbm,
    beta_logit_hbm,
    decay_logit_hbm,
    decay_base_hbm,
    decay_bias_hbm,
    norm_gain_hbm,
    state_scale_hbm,
    arrival_hbm,
    ffn_gain_hbm,
    route_ids_hbm,
    route_weight_hbm,
    out_weight_hbm,
    state_hbm,
    gate_hbm,
    up_hbm,
    down_hbm,
    out,
    residual,
    query,
    keys,
    values,
    out_gate,
    beta_logit,
    decay_logit,
    decay_base,
    decay_bias,
    norm_gain,
    state_scale,
    arrival,
    ffn_gain,
    route_ids,
    route_weight,
    stage,
    small,
    state,
    w_in,
    w_down,
    w_out,
    r0_src,
    r0_in,
    b_src,
    b_in,
    r1_src,
    r1_in,
    g_src,
    g_in,
    p_src,
    p_in,
    c_src,
    c_in,
    k_src,
    k_in,
    n_scr,
    place,
    weigh,
    masks,
    m3_src,
    m3_in,
    x_src,
    x_in,
    h_src,
    h_in,
    m6_src,
    m6_in,
    m7_own,
    m7_src,
    m7_in,
    small_sem,
    load_sem,
    send_sem,
    recv_sem,
):
    count, width = residual_hbm.shape
    chunks = width // LANES
    y_chunks = chunks // ny
    x_chunks = chunks // nx
    key_heads = query_hbm.shape[1] // LANES
    heads = 2 * key_heads
    nz = nzc // 2
    cols = nz * 16
    msg = SRC * chunks
    flat = 16 * chunks
    back = nzc * msg
    groups = nzc // 8
    block = nx * 16

    ep = lax.axis_index("ep")
    my_x = lax.axis_index("tp")
    my_y = ep // nzc
    my_zc = lax.rem(ep, nzc)
    my_z = my_zc // 2
    my_c = lax.rem(my_zc, 2)
    other = 1 - my_c

    def place_of(x, y, z, c):
        return (y * nzc + z * 2 + c, x)

    def at_zc(zc):
        return (my_y * nzc + zc, my_x)

    xs = [lax.rem(my_x + d, nx) for d in range(1, nx)]
    near_first = xs[0:1] + xs[2:] + xs[1:2]
    ys = [lax.rem(my_y + d, ny) for d in range(1, ny)]
    zs = [lax.rem(my_z + d, nz) for d in range(1, nz)]
    zcs = [lax.rem(my_zc + d, nzc) for d in range(1, nzc)]
    sibling = place_of(my_x, my_y, my_z, other)

    sent = []

    def remote(src, dst, hop, target):
        return pltpu.make_async_remote_copy(
            src_ref=src,
            dst_ref=dst,
            send_sem=send_sem.at[hop],
            recv_sem=recv_sem.at[hop],
            device_id=target,
            device_id_type=MESH,
        )

    def send(src, dst, hop, target):
        copy = remote(src, dst, hop, target)
        copy.start()
        sent.append(copy)

    own_cols = pl.ds(pl.multiple_of(my_z * 16, 16), 16)
    smalls = [
        pltpu.make_async_copy(src, dst, small_sem.at[n])
        for n, (src, dst) in enumerate(
            (
                (route_ids_hbm, route_ids),
                (route_weight_hbm, route_weight),
                (residual_hbm, residual),
                (query_hbm, query),
                (keys_hbm, keys),
                (values_hbm, values),
                (out_gate_hbm, out_gate),
                (beta_logit_hbm, beta_logit),
                (decay_logit_hbm, decay_logit),
                (decay_base_hbm, decay_base),
                (decay_bias_hbm, decay_bias),
                (norm_gain_hbm, norm_gain),
                (state_scale_hbm, state_scale),
                (arrival_hbm, arrival),
                (ffn_gain_hbm, ffn_gain),
            )
        )
    ]
    for load in smalls:
        load.start()
    state_load = pltpu.make_async_copy(state_hbm, state, load_sem.at[0])
    state_load.start()
    w_own = pltpu.make_async_copy(out_weight_hbm, w_out.at[own_cols, :], load_sem.at[1])
    w_own.start()

    barrier = pltpu.get_barrier_semaphore()
    peers = [at_zc(zc) for zc in zcs]
    for c in (my_c, other):
        peers += [place_of(my_x, y, my_z, c) for y in ys]
        peers += [place_of(x, my_y, my_z, c) for x in xs]
    for peer in peers:
        pl.semaphore_signal(barrier, inc=1, device_id=peer, device_id_type=MESH)
    pl.semaphore_wait(barrier, len(peers))

    for z in zs:
        send(out_weight_hbm, w_out.at[own_cols, :], 1, place_of(my_x, my_y, z, my_c))

    x_width = x_chunks * LANES
    for x in near_first[0:2]:
        span = pl.ds(pl.multiple_of(x * x_width, x_width), x_width)
        send(down_hbm.at[:, :, span], w_down.at[my_x], 15, place_of(x, my_y, my_z, my_c))

    stage[...] = jnp.zeros_like(stage)
    small[...] = jnp.zeros_like(small)
    q_at, k_at, v_at, g_at = 0, key_heads, 2 * key_heads, 2 * key_heads + heads
    r_at = g_at + heads
    for load in smalls:
        load.wait()
    for at, ref in ((q_at, query), (k_at, keys), (v_at, values), (g_at, out_gate)):
        stage[0:count, at * LANES : at * LANES + ref.shape[1]] = ref[...].astype(F32)
    small[2, 0:count, 0:heads] = decay_logit[...]
    small[3, 0:count, 0:heads] = beta_logit[...]
    rate = jnp.exp(decay_base[...])
    logit = small[2, :, 0:heads] + decay_bias[...]
    soft = jnp.maximum(logit, 0.0) + jnp.log1p(jnp.exp(-jnp.abs(logit)))
    decay = jnp.exp(-rate * soft)
    beta = jax.nn.sigmoid(small[3, :, 0:heads])
    row8 = iota((PAD, 1), 0)
    moved = jnp.zeros((PAD, heads), F32)
    for r in range(count):
        moved = jnp.where(row8 == r, state_scale[pl.ds(arrival[r], 1), :], moved)
    carry = moved * decay
    gain = norm_gain[...]
    state_load.wait()
    for g in range(key_heads):
        q = stage[:, (q_at + g) * LANES : (q_at + g + 1) * LANES]
        k = stage[:, (k_at + g) * LANES : (k_at + g + 1) * LANES]
        q = q * (lax.rsqrt(jnp.sum(q * q, axis=1, keepdims=True) + 1e-06) / math.sqrt(LANES))
        k = k * lax.rsqrt(jnp.sum(k * k, axis=1, keepdims=True) + 1e-06)
        qk = jnp.sum(q * k, axis=1, keepdims=True)
        k_hi = k.astype(BF16).astype(F32)
        q_hi = q.astype(BF16).astype(F32)
        lhs = jnp.concatenate([k_hi, k - k_hi, q_hi, q - q_hi], axis=0).astype(BF16)
        from_k = jnp.zeros((PAD, 2 * LANES), F32)
        from_q = jnp.zeros((PAD, 2 * LANES), F32)
        for r in range(count):
            row = arrival[r]
            both = jnp.concatenate([state[row, 2 * g], state[row, 2 * g + 1]], axis=1)
            got = mm(lhs, both)
            from_k = jnp.where(row8 == r, got[0:8] + got[8:16], from_k)
            from_q = jnp.where(row8 == r, got[16:24] + got[24:32], from_q)
        pair = []
        for i in range(2):
            h = 2 * g + i
            s = carry[:, h : h + 1]
            v = stage[:, (v_at + h) * LANES : (v_at + h + 1) * LANES]
            z = stage[:, (g_at + h) * LANES : (g_at + h + 1) * LANES]
            delta = beta[:, h : h + 1] * (v - s * from_k[:, i * LANES : (i + 1) * LANES])
            o = s * from_q[:, i * LANES : (i + 1) * LANES] + qk * delta
            norm = lax.rsqrt(jnp.mean(o * o, axis=1, keepdims=True) + 1e-06)
            pair.append(o * norm * gain * silu(z))
        g_src[g * 16 : (g + 1) * 16, :] = jnp.concatenate(pair, axis=0).astype(BF16)
    for y in ys:
        for c in (my_c, other):
            send(g_src, g_in.at[my_c * ny + my_y], 2, place_of(my_x, y, my_z, c))
    send(g_src, g_in.at[my_c * ny + my_y], 2, sibling)
    g_in[my_c * ny + my_y] = g_src[...]

    small[0, 0:count, 0:top] = (route_ids[...] + 1).astype(F32)
    small[1, 0:count, 0:top] = route_weight[...]
    r0_src[...] = small[0] + pltpu.roll(small[1], LANES // 2, 1)
    stage[0:count, r_at * LANES : r_at * LANES + width] = residual[...].astype(F32)
    for y in range(ny):
        at = (r_at + y * y_chunks) * LANES
        tiles = [stage[:, at + i * LANES : at + (i + 1) * LANES] for i in range(y_chunks)]
        b_src[y] = jnp.concatenate(tiles, axis=0).astype(BF16)
    for y in ys:
        send(r0_src, r0_in.at[my_y], 0, place_of(my_x, y, my_z, my_c))
        send(b_src.at[y], b_in.at[my_y], 16, place_of(my_x, y, my_z, my_c))
    r0_in[my_y] = r0_src[...]
    b_in[my_y] = b_src[my_y]

    w_loads = []
    for e in range(2):
        for n, ref in ((0, gate_hbm), (2, up_hbm)):
            w_loads.append(
                pltpu.make_async_copy(
                    ref.at[e], w_in.at[:, pl.ds((n + e) * LANES, LANES)], load_sem.at[2 + n + e]
                )
            )
    own_width = pl.ds(pl.multiple_of(my_x * x_width, x_width), x_width)
    w_loads.append(
        pltpu.make_async_copy(down_hbm.at[:, :, own_width], w_down.at[my_x], load_sem.at[6])
    )
    for load in w_loads:
        load.start()

    w_own.wait()
    whole_wait(w_out.at[pl.ds(0, (nz - 1) * 16), :], recv_sem.at[1])
    whole_wait(g_in.at[pl.ds(0, 2 * ny - 1)], recv_sem.at[2])
    first = jnp.zeros((2 * ny * 16, cols), F32)
    second = jnp.zeros((2 * ny * 16, cols), F32)
    for g in range(key_heads):
        rows = g_in[:, g * 16 : (g + 1) * 16, :].reshape(2 * ny * 16, LANES)
        first += mm(rows, w_out[:, 2 * g * LANES : (2 * g + 1) * LANES], NT)
        second += mm(rows, w_out[:, (2 * g + 1) * LANES : (2 * g + 2) * LANES], NT)
    part = first.reshape(2 * ny, 2, PAD, cols)[:, 0] + second.reshape(2 * ny, 2, PAD, cols)[:, 1]
    p_src[...] = part.reshape(2, nx, ROWS, cols)
    for x in xs:
        for c in (my_c, other):
            send(p_src.at[c, x], p_in.at[my_c * nx + my_x], 4, place_of(x, my_y, my_z, c))
    send(p_src.at[other, my_x], p_in.at[my_c * nx + my_x], 4, sibling)
    p_in[my_c * nx + my_x] = p_src[my_c, my_x]
    span = pl.ds(pl.multiple_of(xs[1] * x_width, x_width), x_width)
    send(down_hbm.at[:, :, span], w_down.at[my_x], 15, place_of(xs[1], my_y, my_z, my_c))

    whole_wait(r0_in.at[pl.ds(0, ny - 1)], recv_sem.at[0])
    low = iota((PAD, LANES), 1) < LANES // 2
    ids = jnp.zeros((PAD, LANES), F32)
    picks_w = jnp.zeros((PAD, LANES), F32)
    for y in range(ny):
        both = r0_in[y]
        ids = ids + pltpu.roll(jnp.where(low, both, 0.0), y * top, 1)
        picks_w = picks_w + pltpu.roll(
            jnp.where(low, 0.0, both), (y * top + LANES // 2) % LANES, 1
        )
    r1_src[...] = ids
    for zc in zcs:
        send(r1_src, r1_in.at[my_zc], 3, at_zc(zc))
    r1_in[my_zc] = ids

    def owner_of(t):
        return jnp.floor((t - 1.0) * 0.5).astype(jnp.int32) - my_y * nzc

    sel_row = iota((32, LANES), 0)
    pick = jnp.bitwise_and(sel_row, 15)
    source = SRC * my_x + jnp.right_shift(sel_row, 4)
    sel = ((iota((32, LANES), 1) == source * top + pick) & (pick < top)).astype(F32)
    spread = (iota((PAD, flat), 0) == jnp.bitwise_and(iota((PAD, flat), 1), 7)).astype(F32)
    flat_src = jnp.bitwise_and(jnp.right_shift(iota((16, flat), 1), 3), 1)
    wide = mm(mm(sel, ids, NT, EXACT), spread, precision=EXACT)
    owner = owner_of(jnp.where(flat_src == 0, wide[0:16], wide[16:32]))
    zc_row = iota((nzc, flat), 0)
    hit = jnp.zeros((nzc, flat), F32)
    for j in range(top):
        hit = hit + jnp.where(zc_row == owner[j : j + 1, :], 1.0, 0.0)
    msg_row = iota((msg, flat), 0)
    msg_col = iota((msg, flat), 1)
    match = (jnp.bitwise_and(msg_row, chunks - 1) == jnp.right_shift(msg_col, 4)) & (
        msg_row // chunks == jnp.bitwise_and(jnp.right_shift(msg_col, 3), 1)
    )
    match = match.astype(F32)
    for zc in range(nzc):
        place[zc * msg : (zc + 1) * msg, :] = (hit[zc : zc + 1, :] * match).astype(BF16)

    mixed_rows = ny * x_chunks * PAD
    sel_row = iota((ny * 16, LANES), 0)
    pick = jnp.bitwise_and(sel_row, 15)
    source = jnp.right_shift(sel_row, 4)
    sel = ((iota((ny * 16, LANES), 1) == source * top + pick) & (pick < top)).astype(F32)
    spread = (
        iota((PAD, mixed_rows), 0) == jnp.bitwise_and(iota((PAD, mixed_rows), 1), 7)
    ).astype(F32)
    of_source = iota((16, mixed_rows), 1) // (x_chunks * PAD)

    def table(t):
        wide = mm(mm(sel, t, NT, EXACT), spread, precision=EXACT)
        kept = jnp.zeros((16, mixed_rows), F32)
        for y in range(ny):
            kept = jnp.where(of_source == y, wide[y * 16 : (y + 1) * 16], kept)
        return kept

    owner = owner_of(table(ids))
    weight = table(picks_w)
    zc_row = iota((nzc, mixed_rows), 0)
    hit_w = jnp.zeros((nzc, mixed_rows), F32)
    for j in range(top):
        hit_w = hit_w + jnp.where(zc_row == owner[j : j + 1, :], weight[j : j + 1, :], 0.0)
    weigh_t = hit_w.T
    hi = weigh_t.astype(BF16)
    lo = (weigh_t - hi.astype(F32)).astype(BF16)
    open_up = (iota((nzc, back), 0) == iota((nzc, back), 1) // msg).astype(BF16)
    w_row = iota((mixed_rows, back), 0)
    w_col = iota((mixed_rows, back), 1)
    kept = jnp.right_shift(w_row, 3) == jnp.bitwise_and(w_col, msg - 1)
    weigh[0] = jnp.where(kept, mm(hi, open_up), 0.0).astype(BF16)
    weigh[1] = jnp.where(kept, mm(lo, open_up), 0.0).astype(BF16)

    mix_row = iota((2 * cols, 2 * cols), 0)
    mix_col = iota((2 * cols, 2 * cols), 1)
    mix = (
        (mix_row // cols == jnp.bitwise_and(jnp.right_shift(mix_col, 4), 1))
        & (
            jnp.right_shift(jnp.bitwise_and(mix_row, cols - 1), 4)
            == jnp.right_shift(mix_col, 5)
        )
        & (jnp.bitwise_and(mix_row, 15) == jnp.bitwise_and(mix_col, 15))
    )
    mix = mix.astype(BF16)

    whole_wait(b_in.at[pl.ds(0, ny - 1)], recv_sem.at[16])
    whole_wait(p_in.at[pl.ds(0, 2 * nx - 1)], recv_sem.at[4])
    attn = []
    for c in range(2):
        total = p_in[c * nx]
        for x in range(1, nx):
            total = total + p_in[c * nx + x]
        attn.append(total.astype(BF16))
    attn = mm(jnp.concatenate(attn, axis=1), mix)
    base_rows = [b_in[SRC * my_x + s].astype(F32) for s in range(SRC)]
    for i in range(y_chunks):
        base = jnp.concatenate([rows[i * PAD : (i + 1) * PAD] for rows in base_rows], axis=0)
        c_src[i] = (base + attn[:, i * LANES : (i + 1) * LANES]).astype(BF16)
    for y in ys:
        send(c_src, c_in.at[my_y], 5, place_of(my_x, y, my_z, my_c))
    c_in[my_y] = c_src[...]

    whole_wait(r1_in.at[pl.ds(0, nzc - 1)], recv_sem.at[3])
    slot = iota((groups * block, nzc), 0)
    slot_zc = (slot // block) * 8 + jnp.bitwise_and(jnp.right_shift(slot, 1), 7)
    of_zc = (slot_zc == iota((groups * block, nzc), 1)).astype(BF16)
    slot = iota((groups * block, LANES), 0)
    slot_x = jnp.right_shift(jnp.bitwise_and(slot, block - 1), 4)
    slot_y = SRC * slot_x + jnp.bitwise_and(slot, 1)
    lane = iota((groups * block, LANES), 1)
    of_y = (lane >= slot_y * top) & (lane < slot_y * top + top)
    arrived = r1_in[...]
    for e in range(2):
        named = (2 * ep + 1 + e).astype(F32)
        found = jnp.sum(jnp.where(arrived == named, 1.0, 0.0), axis=1).astype(BF16)
        found = jnp.where(of_y, mm(of_zc, found), 0.0)
        masks[e] = jnp.broadcast_to(
            jnp.sum(found, axis=1, keepdims=True), (groups * block, LANES)
        )

    whole_wait(c_in.at[pl.ds(0, ny - 1)], recv_sem.at[5])
    squares = jnp.zeros((ROWS, LANES), F32)
    for ch in range(chunks):
        c = c_in[ch // y_chunks, ch % y_chunks].astype(F32)
        squares = squares + c * c
    norm = lax.rsqrt(jnp.sum(squares, axis=1, keepdims=True) / width + 1e-06)
    for ch in range(chunks):
        c = c_in[ch // y_chunks, ch % y_chunks].astype(F32)
        n_scr[ch * 16 : (ch + 1) * 16, :] = (
            c * norm * ffn_gain[:, ch * LANES : (ch + 1) * LANES]
        ).astype(BF16)

    m3_src[...] = mm(place[...], n_scr[...]).astype(BF16).reshape(nzc, msg, LANES)
    my_group = my_zc // 8
    for zc in zcs:
        send(m3_src.at[zc], m3_in.at[my_zc], 6 + my_group, at_zc(zc))
    m3_own = pltpu.make_async_copy(m3_src.at[my_zc], m3_in.at[my_zc], recv_sem.at[6 + my_group])
    m3_own.start()

    half = my_y - SRC * my_x
    home = (half >= 0) & (half < SRC)
    for x in range(nx):
        tiles = []
        for ch in range(x * x_chunks, (x + 1) * x_chunks):
            c = c_in[ch // y_chunks, ch % y_chunks].astype(F32)
            tiles.append(jnp.where(half == 0, c[0:PAD], c[PAD : 2 * PAD]))
        k_src[x] = jnp.concatenate(tiles, axis=0).astype(BF16)
    k_away = [remote(k_src.at[x], k_in, 14, place_of(x, my_y, my_z, my_c)) for x in xs]
    k_own = pltpu.make_async_copy(k_src.at[my_x], k_in, recv_sem.at[14])

    @pl.when(home)
    def _():
        k_own.start()
        for copy in k_away:
            copy.start()

    turn_row = iota((flat, flat), 0)
    turn_col = iota((flat, flat), 1)
    unflat = (jnp.bitwise_and(turn_row, 15) == turn_col // chunks) & (
        jnp.right_shift(turn_row, 4) == jnp.bitwise_and(turn_col, chunks - 1)
    )
    unflat = unflat.astype(BF16)
    for n in range(groups):
        whole_wait(m3_in.at[pl.ds(n * 8, 8)], recv_sem.at[6 + n])
        turned = mm(unflat, m3_in[n * 8 : (n + 1) * 8].reshape(flat, LANES)).astype(BF16)
        for ch in range(chunks):
            x_src[n, :, ch * LANES : (ch + 1) * LANES] = turned[ch * 16 : (ch + 1) * 16]
        for x in near_first:
            send(x_src.at[n], x_in.at[n, my_x], 8 + n, place_of(x, my_y, my_z, my_c))
        x_in[n, my_x] = x_src[n]

    for load in w_loads:
        load.wait()
    for n in range(groups):
        whole_wait(x_in.at[n, pl.ds(0, nx - 1)], recv_sem.at[8 + n])
        both = mm(x_in[n].reshape(block, width), w_in[...])
        hidden = jnp.zeros((block, LANES), F32)
        for e in range(2):
            gate = both[:, e * LANES : (e + 1) * LANES]
            up = both[:, (2 + e) * LANES : (3 + e) * LANES]
            hidden = hidden + silu(gate) * up * masks[e, n * block : (n + 1) * block]
        h_src[n] = hidden.astype(BF16)
        for x in xs:
            send(h_src.at[n], h_in.at[n, my_x], 10 + n, place_of(x, my_y, my_z, my_c))
        h_in[n, my_x] = h_src[n]

    back_row = iota((block * x_chunks, block * x_chunks), 0)
    back_col = iota((block * x_chunks, block * x_chunks), 1)
    row_y = (back_row % msg) // x_chunks
    slot = jnp.bitwise_and(back_col, 15)
    flatten = (
        (back_row // msg == jnp.right_shift(slot, 1))
        & (row_y == SRC * (back_col // (16 * x_chunks)) + jnp.bitwise_and(slot, 1))
        & (back_row % x_chunks == jnp.right_shift(back_col, 4) % x_chunks)
    )
    flatten = flatten.astype(BF16)
    whole_wait(w_down.at[pl.ds(0, nx - 1)], recv_sem.at[15])
    for n in range(groups):
        whole_wait(h_in.at[n, pl.ds(0, nx - 1)], recv_sem.at[10 + n])
        total = jnp.zeros((block, x_width), F32)
        for x in range(nx):
            h = h_in[n, x].astype(F32)
            for e in range(2):
                chosen = (h * masks[e, n * block : (n + 1) * block]).astype(BF16)
                total = total + mm(chosen, w_down[x, e])
        total = total.astype(BF16)
        tiles = [
            total[x * 16 : (x + 1) * 16, ch * LANES : (ch + 1) * LANES]
            for x in range(nx)
            for ch in range(x_chunks)
        ]
        turned = mm(flatten, jnp.concatenate(tiles, axis=0)).astype(BF16)
        m6_src[n * 8 : (n + 1) * 8] = turned.reshape(8, msg, LANES)
        for i in range(8):
            zc = n * 8 + i
            away = remote(m6_src.at[zc], m6_in.at[my_zc], 12, at_zc(zc))
            keep = pltpu.make_async_copy(m6_src.at[zc], m6_in.at[my_zc], recv_sem.at[12])

            @pl.when(zc == my_zc)
            def _():
                keep.start()

            @pl.when(zc != my_zc)
            def _():
                away.start()

    whole_wait(m6_in, recv_sem.at[12])
    rows = m6_in[...].reshape(back, LANES)
    mixed = (mm(weigh[0], rows) + mm(weigh[1], rows)).reshape(ny, x_chunks * PAD, LANES)
    m7_own[...] = mixed
    m7_src[...] = mixed.astype(BF16)
    for y in ys:
        send(m7_src.at[y], m7_in.at[my_y], 13, place_of(my_x, y, my_z, my_c))

    for copy in sent:
        copy.wait_send()
    whole_wait(m6_src.at[pl.ds(0, nzc - 1)], send_sem.at[12])

    @pl.when(home)
    def _():
        for copy in k_away:
            copy.wait_send()

    whole_wait(k_in, recv_sem.at[14])
    whole_wait(m7_in.at[pl.ds(0, ny - 1)], recv_sem.at[13])
    total = m7_own[my_y]
    for y in ys:
        total = total + m7_in[y].astype(F32)
    total = (total + k_in[...].astype(F32)).reshape(x_chunks, PAD, LANES)
    for i in range(x_chunks):
        out[:, i * LANES : (i + 1) * LANES] = total[i, 0:count].astype(BF16)


def shards(
    nx,
    ny,
    nzc,
    residual_in,
    new_query,
    new_keys,
    new_values,
    out_gate,
    beta_logit,
    decay_logit,
    decay_base,
    decay_bias,
    norm_gain,
    state_store,
    state_scale,
    arrival,
    out_weight,
    ffn_gain,
    expert_gate_weight,
    expert_up_weight,
    expert_down_weight,
    route_ids,
    route_weight,
):
    count, width = residual_in.shape
    key_heads = new_query.shape[1] // LANES
    heads = 2 * key_heads
    top = route_ids.shape[1]
    chunks = width // LANES
    y_chunks = chunks // ny
    x_chunks = chunks // nx
    msg = SRC * chunks
    flat = 16 * chunks
    cols = nzc // 2 * 16
    groups = nzc // 8
    block = nx * 16
    stage_tiles = 2 * key_heads + 2 * heads + chunks
    vmem = pl.BlockSpec(memory_space=pltpu.VMEM)
    hbm = pl.BlockSpec(memory_space=pltpu.HBM)
    small_operands = (
        residual_in,
        new_query,
        new_keys,
        new_values,
        out_gate,
        beta_logit,
        decay_logit,
        decay_base[None, :],
        decay_bias[None, :],
        norm_gain[None, :],
        state_scale,
        arrival,
        ffn_gain[None, :],
        route_ids,
        route_weight,
    )
    scratch = [
        (pltpu.SMEM if a is arrival else pltpu.VMEM)(a.shape, a.dtype) for a in small_operands
    ] + [
        pltpu.VMEM((PAD, stage_tiles * LANES), F32),
        pltpu.VMEM((4, PAD, LANES), F32),
        pltpu.VMEM(state_store.shape, BF16),
        pltpu.VMEM((width, 4 * LANES), BF16),
        pltpu.VMEM((nx, 2, LANES, width // nx), BF16),
        pltpu.VMEM((cols, heads * LANES), BF16),
        pltpu.VMEM((PAD, LANES), F32),
        pltpu.VMEM((ny, PAD, LANES), F32),
        pltpu.VMEM((ny, y_chunks * PAD, LANES), BF16),
        pltpu.VMEM((ny, y_chunks * PAD, LANES), BF16),
        pltpu.VMEM((PAD, LANES), F32),
        pltpu.VMEM((nzc, PAD, LANES), F32),
        pltpu.VMEM((heads * PAD, LANES), BF16),
        pltpu.VMEM((2 * ny, heads * PAD, LANES), BF16),
        pltpu.VMEM((2, nx, ROWS, cols), F32),
        pltpu.VMEM((2 * nx, ROWS, cols), F32),
        pltpu.VMEM((y_chunks, ROWS, LANES), BF16),
        pltpu.VMEM((ny, y_chunks, ROWS, LANES), BF16),
        pltpu.VMEM((nx, x_chunks * PAD, LANES), BF16),
        pltpu.VMEM((x_chunks * PAD, LANES), BF16),
        pltpu.VMEM((flat, LANES), BF16),
        pltpu.VMEM((nzc * msg, flat), BF16),
        pltpu.VMEM((2, ny * x_chunks * PAD, nzc * msg), BF16),
        pltpu.VMEM((2, groups * block, LANES), F32),
        pltpu.VMEM((nzc, msg, LANES), BF16),
        pltpu.VMEM((nzc, msg, LANES), BF16),
        pltpu.VMEM((groups, 16, width), BF16),
        pltpu.VMEM((groups, nx, 16, width), BF16),
        pltpu.VMEM((groups, block, LANES), BF16),
        pltpu.VMEM((groups, nx, block, LANES), BF16),
        pltpu.VMEM((nzc, msg, LANES), BF16),
        pltpu.VMEM((nzc, msg, LANES), BF16),
        pltpu.VMEM((ny, x_chunks * PAD, LANES), F32),
        pltpu.VMEM((ny, x_chunks * PAD, LANES), BF16),
        pltpu.VMEM((ny, x_chunks * PAD, LANES), BF16),
        pltpu.SemaphoreType.DMA((len(small_operands),)),
        pltpu.SemaphoreType.DMA((8,)),
        pltpu.SemaphoreType.DMA((17,)),
        pltpu.SemaphoreType.DMA((17,)),
    ]
    return pl.pallas_call(
        functools.partial(kernel, nx, ny, nzc, top),
        out_shape=jax.ShapeDtypeStruct((count, width // nx), BF16),
        in_specs=[hbm] * (len(small_operands) + 5),
        out_specs=vmem,
        scratch_shapes=scratch,
        compiler_params=pltpu.CompilerParams(
            collective_id=0, has_side_effects=True, vmem_limit_bytes=60 * 1024 * 1024
        ),
        name="decode_layer",
    )(
        *small_operands,
        out_weight.T,
        state_store,
        expert_gate_weight,
        expert_up_weight,
        expert_down_weight,
    )


def solution(mesh):
    nx = mesh.shape["tp"]
    ny = SRC * nx
    nzc = mesh.shape["ep"] // ny
    return jax.shard_map(
        functools.partial(shards, nx, ny, nzc),
        mesh=mesh,
        in_specs=(
            P("ep", None),
            P("ep", "tp"),
            P("ep", "tp"),
            P("ep", "tp"),
            P("ep", "tp"),
            P("ep", "tp"),
            P("ep", "tp"),
            P("tp"),
            P("tp"),
            P(),
            P("ep", "tp", None, None),
            P("ep", "tp"),
            P("ep"),
            P("tp", "ep"),
            P(),
            P("ep", None, "tp"),
            P("ep", None, "tp"),
            P("ep", "tp", None),
            P("ep", None),
            P("ep", None),
        ),
        out_specs=P("ep", "tp"),
        check_vma=False,
    )
```

```python
import functools
import math

import jax
import jax.numpy as jnp
from jax import lax
from jax.experimental import pallas as pl
from jax.experimental.pallas import tpu as pltpu
from jax.sharding import PartitionSpec as P

MESH = pl.DeviceIdType.MESH
F32 = jnp.float32
BF16 = jnp.bfloat16
LANES = 128
PAD = 8
SRC = 2
Z_ORDER = (0, 1, 7, 2, 6, 3, 5, 4)
Y_ORDER = (4, 3, 5, 2, 6, 1, 7, 0)
ROWS = SRC * PAD
NT = (((1,), (1,)), ((), ()))
EXACT = lax.Precision.HIGHEST


def mm(a, b, dims=(((1,), (0,)), ((), ())), precision=None):
    return lax.dot_general(a, b, dims, preferred_element_type=F32, precision=precision)


def iota(shape, axis):
    return lax.broadcasted_iota(jnp.int32, shape, axis)


def silu(v):
    return v * jax.nn.sigmoid(v)


def whole_wait(ref, sem):
    pltpu.make_async_copy(ref, ref, sem).wait()


def kernel(
    nx,
    ny,
    nzc,
    top,
    residual_hbm,
    query_hbm,
    keys_hbm,
    values_hbm,
    out_gate_hbm,
    beta_logit_hbm,
    decay_logit_hbm,
    decay_base_hbm,
    decay_bias_hbm,
    norm_gain_hbm,
    state_scale_hbm,
    arrival_hbm,
    ffn_gain_hbm,
    route_ids_hbm,
    route_weight_hbm,
    out_weight_hbm,
    state_hbm,
    gate_hbm,
    up_hbm,
    down_hbm,
    out,
    residual,
    query,
    keys,
    values,
    out_gate,
    beta_logit,
    decay_logit,
    decay_base,
    decay_bias,
    norm_gain,
    state_scale,
    arrival,
    ffn_gain,
    route_ids,
    route_weight,
    stage,
    small,
    state,
    w_in,
    w_down,
    w_out,
    r0_src,
    r0_in,
    b_src,
    b_in,
    r1_src,
    r1_in,
    g_pad,
    g_src,
    g_in,
    g_all,
    p_src,
    p_in,
    k_src,
    k_in,
    place,
    weigh,
    masks,
    m3_src,
    m3_in,
    x_src,
    x_in,
    h_src,
    h_in,
    m6_src,
    m6_in,
    small_sem,
    load_sem,
    send_sem,
    recv_sem,
):
    count, width = residual_hbm.shape
    chunks = width // LANES
    y_chunks = chunks // ny
    x_chunks = chunks // nx
    key_heads = query_hbm.shape[1] // LANES
    heads = 2 * key_heads
    nz = nzc // 2
    cols = nz * 16
    msg = SRC * chunks
    flat = 16 * chunks
    owners = ny * nzc
    back = owners * 4
    groups = nzc // 8
    block = nx * 16

    ep = lax.axis_index("ep")
    my_x = lax.axis_index("tp")
    my_y = ep // nzc
    my_zc = lax.rem(ep, nzc)
    my_z = my_zc // 2
    my_c = lax.rem(my_zc, 2)
    other = 1 - my_c

    def place_of(x, y, z, c):
        return (y * nzc + z * 2 + c, x)

    def at_zc(zc):
        return (my_y * nzc + zc, my_x)

    xs = [lax.rem(my_x + d, nx) for d in range(1, nx)]
    near_first = xs[0:1] + xs[2:] + xs[1:2]
    ys = [lax.rem(my_y + d, ny) for d in range(1, ny)]
    zs = [lax.rem(my_z + d, nz) for d in range(1, nz)]
    zcs = [lax.rem(my_zc + d, nzc) for d in range(1, nzc)]
    sibling = place_of(my_x, my_y, my_z, other)

    order = Z_ORDER
    z_from = [lax.rem(my_z + d, nz) for d in order]
    z_to = [lax.rem(my_z + nz - d, nz) for d in order]

    sent = []

    def remote(src, dst, hop, target):
        return pltpu.make_async_remote_copy(
            src_ref=src,
            dst_ref=dst,
            send_sem=send_sem.at[hop],
            recv_sem=recv_sem.at[hop],
            device_id=target,
            device_id_type=MESH,
        )

    def send(src, dst, hop, target):
        copy = remote(src, dst, hop, target)
        copy.start()
        sent.append(copy)

    own_cols = pl.ds(pl.multiple_of(my_z * 16, 16), 16)
    smalls = [
        pltpu.make_async_copy(src, dst, small_sem.at[n])
        for n, (src, dst) in enumerate(
            (
                (route_ids_hbm, route_ids),
                (route_weight_hbm, route_weight),
                (residual_hbm, residual),
                (query_hbm, query),
                (keys_hbm, keys),
                (values_hbm, values),
                (out_gate_hbm, out_gate),
                (beta_logit_hbm, beta_logit),
                (decay_logit_hbm, decay_logit),
                (decay_base_hbm, decay_base),
                (decay_bias_hbm, decay_bias),
                (norm_gain_hbm, norm_gain),
                (state_scale_hbm, state_scale),
                (arrival_hbm, arrival),
                (ffn_gain_hbm, ffn_gain),
            )
        )
    ]
    for load in smalls:
        load.start()
    state_load = pltpu.make_async_copy(state_hbm, state, load_sem.at[0])
    state_load.start()
    w_own = pltpu.make_async_copy(out_weight_hbm, w_out.at[own_cols, :], load_sem.at[1])
    w_own.start()

    barrier = pltpu.get_barrier_semaphore()
    peers = [at_zc(zc) for zc in zcs]
    for c in (my_c, other):
        peers += [place_of(my_x, y, my_z, c) for y in ys]
        peers += [place_of(x, my_y, my_z, c) for x in xs]
    for peer in peers:
        pl.semaphore_signal(barrier, inc=1, device_id=peer, device_id_type=MESH)
    pl.semaphore_wait(barrier, len(peers))

    for z in zs:
        send(out_weight_hbm, w_out.at[own_cols, :], 1, place_of(my_x, my_y, z, my_c))

    x_width = x_chunks * LANES
    for x in near_first[0:2]:
        span = pl.ds(pl.multiple_of(x * x_width, x_width), x_width)
        send(down_hbm.at[:, :, span], w_down.at[my_x], 15, place_of(x, my_y, my_z, my_c))

    stage[...] = jnp.zeros_like(stage)
    small[...] = jnp.zeros_like(small)
    q_at, k_at, v_at, g_at = 0, key_heads, 2 * key_heads, 2 * key_heads + heads
    r_at = g_at + heads
    for load in smalls:
        load.wait()
    for at, ref in ((q_at, query), (k_at, keys), (v_at, values), (g_at, out_gate)):
        stage[0:count, at * LANES : at * LANES + ref.shape[1]] = ref[...].astype(F32)
    small[2, 0:count, 0:heads] = decay_logit[...]
    small[3, 0:count, 0:heads] = beta_logit[...]
    rate = jnp.exp(decay_base[...])
    logit = small[2, :, 0:heads] + decay_bias[...]
    soft = jnp.maximum(logit, 0.0) + jnp.log1p(jnp.exp(-jnp.abs(logit)))
    decay = jnp.exp(-rate * soft)
    beta = jax.nn.sigmoid(small[3, :, 0:heads])
    row8 = iota((PAD, 1), 0)
    moved = jnp.zeros((PAD, heads), F32)
    for r in range(count):
        moved = jnp.where(row8 == r, state_scale[pl.ds(arrival[r], 1), :], moved)
    carry = moved * decay
    gain = norm_gain[...]
    state_load.wait()
    for g in range(key_heads):
        q = stage[:, (q_at + g) * LANES : (q_at + g + 1) * LANES]
        k = stage[:, (k_at + g) * LANES : (k_at + g + 1) * LANES]
        q = q * (lax.rsqrt(jnp.sum(q * q, axis=1, keepdims=True) + 1e-06) / math.sqrt(LANES))
        k = k * lax.rsqrt(jnp.sum(k * k, axis=1, keepdims=True) + 1e-06)
        qk = jnp.sum(q * k, axis=1, keepdims=True)
        k_hi = k.astype(BF16).astype(F32)
        q_hi = q.astype(BF16).astype(F32)
        lhs = jnp.concatenate([k_hi, k - k_hi, q_hi, q - q_hi], axis=0).astype(BF16)
        from_k = jnp.zeros((PAD, 2 * LANES), F32)
        from_q = jnp.zeros((PAD, 2 * LANES), F32)
        for r in range(count):
            row = arrival[r]
            both = jnp.concatenate([state[row, 2 * g], state[row, 2 * g + 1]], axis=1)
            got = mm(lhs, both)
            from_k = jnp.where(row8 == r, got[0:8] + got[8:16], from_k)
            from_q = jnp.where(row8 == r, got[16:24] + got[24:32], from_q)
        pair = []
        for i in range(2):
            h = 2 * g + i
            s = carry[:, h : h + 1]
            v = stage[:, (v_at + h) * LANES : (v_at + h + 1) * LANES]
            z = stage[:, (g_at + h) * LANES : (g_at + h + 1) * LANES]
            delta = beta[:, h : h + 1] * (v - s * from_k[:, i * LANES : (i + 1) * LANES])
            o = s * from_q[:, i * LANES : (i + 1) * LANES] + qk * delta
            norm = lax.rsqrt(jnp.mean(o * o, axis=1, keepdims=True) + 1e-06)
            pair.append(o * norm * gain * silu(z))
        g_pad[g * 16 : (g + 1) * 16, :] = jnp.concatenate(pair, axis=0).astype(BF16)
    row = iota((count * heads, heads * PAD), 0)
    col = iota((count * heads, heads * PAD), 1)
    filled = jnp.bitwise_and(col, 7) < count
    pack = (row == jnp.right_shift(col, 3) * count + jnp.bitwise_and(col, 7)) & filled
    g_src[...] = mm(pack.astype(BF16), g_pad[...]).astype(BF16)
    for y in ys:
        for c in (my_c, other):
            send(g_src, g_in.at[my_c * ny + my_y], 2, place_of(my_x, y, my_z, c))
    send(g_src, g_in.at[my_c * ny + my_y], 2, sibling)
    g_in[my_c * ny + my_y] = g_src[...]

    small[0, 0:count, 0:top] = (route_ids[...] + 1).astype(F32)
    small[1, 0:count, 0:top] = route_weight[...]
    r0_src[...] = pltpu.roll(small[0], my_y * top, 1)
    stage[0:count, r_at * LANES : r_at * LANES + width] = residual[...].astype(F32)
    for y in range(ny):
        at = (r_at + y * y_chunks) * LANES
        tiles = [stage[:, at + i * LANES : at + (i + 1) * LANES] for i in range(y_chunks)]
        b_src[y] = jnp.concatenate(tiles, axis=0).astype(BF16)
    for y in ys:
        send(r0_src, r0_in.at[my_y], 0, place_of(my_x, y, my_z, my_c))
        send(b_src.at[y], b_in.at[my_y], 16, place_of(my_x, y, my_z, my_c))
    r0_in[my_y] = r0_src[...]
    b_in[my_y] = b_src[my_y]

    w_loads = []
    for e in range(2):
        for n, ref in ((0, gate_hbm), (2, up_hbm)):
            w_loads.append(
                pltpu.make_async_copy(
                    ref.at[e], w_in.at[:, pl.ds((n + e) * LANES, LANES)], load_sem.at[2 + n + e]
                )
            )
    own_width = pl.ds(pl.multiple_of(my_x * x_width, x_width), x_width)
    w_loads.append(
        pltpu.make_async_copy(down_hbm.at[:, :, own_width], w_down.at[my_x], load_sem.at[6])
    )
    for load in w_loads:
        load.start()

    w_own.wait()
    whole_wait(w_out.at[pl.ds(0, (nz - 1) * 16), :], recv_sem.at[1])
    row = iota((4 * heads * PAD, 4 * heads * count), 0)
    col = iota((4 * heads * PAD, 4 * heads * count), 1)
    filled = jnp.bitwise_and(row, 7) < count
    unpack = (col == jnp.right_shift(row, 3) * count + jnp.bitwise_and(row, 7)) & filled
    unpack = unpack.astype(BF16)
    whole_wait(g_in.at[pl.ds(0, 2 * ny - 1)], recv_sem.at[2])
    for n in range(0, 2 * ny, 4):
        four = mm(unpack, g_in[n : n + 4].reshape(4 * heads * count, LANES))
        g_all[n : n + 4] = four.astype(BF16).reshape(4, heads * PAD, LANES)
    first = jnp.zeros((2 * ny * 16, cols), F32)
    second = jnp.zeros((2 * ny * 16, cols), F32)
    for g in range(key_heads):
        rows = g_all[:, g * 16 : (g + 1) * 16, :].reshape(2 * ny * 16, LANES)
        first += mm(rows, w_out[:, 2 * g * LANES : (2 * g + 1) * LANES], NT)
        second += mm(rows, w_out[:, (2 * g + 1) * LANES : (2 * g + 2) * LANES], NT)
    part = first.reshape(2 * ny, 2, PAD, cols)[:, 0] + second.reshape(2 * ny, 2, PAD, cols)[:, 1]
    p_src[...] = part.reshape(2, nx, ROWS, cols)
    for x in xs:
        for c in (my_c, other):
            send(p_src.at[c, x], p_in.at[my_c * nx + my_x], 4, place_of(x, my_y, my_z, c))
    send(p_src.at[other, my_x], p_in.at[my_c * nx + my_x], 4, sibling)
    p_in[my_c * nx + my_x] = p_src[my_c, my_x]
    whole_wait(r0_in.at[pl.ds(0, ny - 1)], recv_sem.at[0])
    ids = jnp.sum(r0_in[...], axis=0)
    r1_src[...] = ids
    for zc in zcs:
        send(r1_src, r1_in.at[my_zc], 3, at_zc(zc))
    r1_in[my_zc] = ids

    here = y_chunks * ROWS
    sel_row = iota((32, LANES), 0)
    pick = jnp.bitwise_and(sel_row, 15)
    source = SRC * my_x + jnp.right_shift(sel_row, 4)
    sel = ((iota((32, LANES), 1) == source * top + pick) & (pick < top)).astype(F32)
    spread = (iota((PAD, here), 0) == jnp.bitwise_and(iota((PAD, here), 1), 7)).astype(F32)
    of_source = jnp.bitwise_and(jnp.right_shift(iota((16, here), 1), 3), 1)
    wide = mm(mm(sel, ids, NT, EXACT), spread, precision=EXACT)
    owner = jnp.where(of_source == 0, wide[0:16], wide[16:32])
    owner = jnp.floor((owner - 1.0) * 0.5).astype(jnp.int32)
    owner_row = iota((owners, here), 0)
    hit = jnp.zeros((owners, here), F32)
    for j in range(top):
        hit = hit + jnp.where(owner_row == owner[j : j + 1, :], 1.0, 0.0)
    each = (iota((owners * 4, owners), 1) == jnp.right_shift(iota((owners * 4, owners), 0), 2))
    row = iota((owners * 4, here), 0)
    col = iota((owners * 4, here), 1)
    match = (jnp.bitwise_and(jnp.right_shift(row, 1), 1) == jnp.bitwise_and(jnp.right_shift(col, 3), 1)) & (
        jnp.bitwise_and(row, 1) == jnp.right_shift(col, 4)
    )
    place[...] = jnp.where(match, mm(each.astype(BF16), hit.astype(BF16)), 0.0).astype(BF16)

    own_ids = small[0]
    own_weight = small[1]
    lane = iota((PAD, LANES), 1)
    share = jnp.zeros((PAD, owners), F32)
    for j in range(top):
        named = jnp.floor((own_ids[:, j : j + 1] - 1.0) * 0.5).astype(jnp.int32)
        share = share + jnp.where(lane == named, own_weight[:, j : j + 1], 0.0)
    hi = share.astype(BF16).astype(F32)
    open_up = iota((owners, back), 0) == jnp.right_shift(iota((owners, back), 1), 2)
    both = mm(jnp.concatenate([hi, share - hi], axis=0).astype(BF16), open_up.astype(BF16))
    row = iota((x_chunks * PAD, back), 0)
    kept = jnp.right_shift(row, 3) == jnp.bitwise_and(iota((x_chunks * PAD, back), 1), 3)
    for n in range(2):
        tall = jnp.concatenate([both[n * PAD : (n + 1) * PAD]] * x_chunks, axis=0)
        weigh[n] = jnp.where(kept, tall, 0.0).astype(BF16)

    mix_row = iota((2 * cols, 2 * cols), 0)
    mix_col = iota((2 * cols, 2 * cols), 1)
    mix = (
        (mix_row // cols == jnp.bitwise_and(jnp.right_shift(mix_col, 4), 1))
        & (
            jnp.right_shift(jnp.bitwise_and(mix_row, cols - 1), 4)
            == jnp.right_shift(mix_col, 5)
        )
        & (jnp.bitwise_and(mix_row, 15) == jnp.bitwise_and(mix_col, 15))
    )
    mix = mix.astype(BF16)

    whole_wait(b_in.at[pl.ds(0, ny - 1)], recv_sem.at[16])
    whole_wait(p_in.at[pl.ds(0, 2 * nx - 1)], recv_sem.at[4])
    attn = []
    for c in range(2):
        total = p_in[c * nx]
        for x in range(1, nx):
            total = total + p_in[c * nx + x]
        attn.append(total.astype(BF16))
    attn = mm(jnp.concatenate(attn, axis=1), mix)
    base_rows = [b_in[SRC * my_x + s].astype(F32) for s in range(SRC)]
    parts = []
    for i in range(y_chunks):
        base = jnp.concatenate([rows[i * PAD : (i + 1) * PAD] for rows in base_rows], axis=0)
        parts.append(base + attn[:, i * LANES : (i + 1) * LANES])
    carried = jnp.concatenate(parts, axis=0).astype(BF16)

    m3_src[...] = mm(place[...], carried).astype(BF16).reshape(owners, 4, LANES)
    for i, z in enumerate(z_to):
        for c in (my_c, other):
            for dy in Y_ORDER:
                y = lax.rem(my_y + dy, ny)
                to = place_of(my_x, y, z, c)
                src = m3_src.at[to[0]]
                dst = m3_in.at[i * 2 + my_c, my_y]
                if order[i] or dy or c is other:
                    send(src, dst, 6 + i // 4, to)
                else:
                    pltpu.make_async_copy(src, dst, recv_sem.at[6 + i // 4]).start()

    half = my_y - SRC * my_x
    wide = carried.astype(F32)
    to_x = my_y // SRC
    k_dst = k_in.at[my_y - SRC * to_x]
    k_copies = []
    for n in range(SRC):
        rows = [wide[i * ROWS + n * PAD : i * ROWS + (n + 1) * PAD] for i in range(y_chunks)]
        k_src[n] = jnp.concatenate(rows, axis=0).astype(BF16)
        away = remote(k_src.at[n], k_dst, 14, place_of(to_x, SRC * my_x + n, my_z, my_c))
        keep = pltpu.make_async_copy(k_src.at[n], k_dst, recv_sem.at[14])
        k_copies.append(away)

        @pl.when(half == n)
        def _():
            keep.start()

        @pl.when(half != n)
        def _():
            away.start()

    span = pl.ds(pl.multiple_of(xs[1] * x_width, x_width), x_width)
    send(down_hbm.at[:, :, span], w_down.at[my_x], 15, place_of(xs[1], my_y, my_z, my_c))

    whole_wait(r1_in.at[pl.ds(0, nzc - 1)], recv_sem.at[3])
    slot = iota((groups * block, nzc), 0)
    slot_i = (slot // block) * 4 + jnp.bitwise_and(jnp.right_shift(slot, 2), 3)
    slot_z = jnp.zeros_like(slot)
    for i, z in enumerate(z_from):
        slot_z = jnp.where(slot_i == i, z, slot_z)
    slot_zc = slot_z * 2 + jnp.bitwise_and(jnp.right_shift(slot, 1), 1)
    of_zc = (slot_zc == iota((groups * block, nzc), 1)).astype(BF16)
    slot = iota((groups * block, LANES), 0)
    slot_x = jnp.right_shift(jnp.bitwise_and(slot, block - 1), 4)
    slot_y = SRC * slot_x + jnp.bitwise_and(slot, 1)
    lane = iota((groups * block, LANES), 1)
    of_y = (lane >= slot_y * top) & (lane < slot_y * top + top)
    arrived = r1_in[...]
    for e in range(2):
        named = (2 * ep + 1 + e).astype(F32)
        found = jnp.sum(jnp.where(arrived == named, 1.0, 0.0), axis=1).astype(BF16)
        found = jnp.where(of_y, mm(of_zc, found), 0.0)
        masks[e] = jnp.broadcast_to(
            jnp.sum(found, axis=1, keepdims=True), (groups * block, LANES)
        )

    turn_row = iota((flat, flat), 0)
    turn_col = iota((flat, flat), 1)
    turn_ch = jnp.right_shift(turn_row, 4)
    turn_slot = jnp.bitwise_and(turn_row, 15)
    unflat = turn_col == (
        (turn_slot // 2) * (ny * 4)
        + (turn_ch // y_chunks) * 4
        + jnp.bitwise_and(turn_slot, 1) * y_chunks
        + turn_ch % y_chunks
    )
    unflat = unflat.astype(BF16)
    for n in range(groups):
        whole_wait(m3_in.at[pl.ds(n * 8, 8)], recv_sem.at[6 + n])
        turned = mm(unflat, m3_in[n * 8 : (n + 1) * 8].reshape(flat, LANES))
        squares = jnp.zeros((16, LANES), F32)
        for ch in range(chunks):
            c = turned[ch * 16 : (ch + 1) * 16]
            squares = squares + c * c
        norm = lax.rsqrt(jnp.sum(squares, axis=1, keepdims=True) / width + 1e-06)
        for ch in range(chunks):
            c = turned[ch * 16 : (ch + 1) * 16]
            span = slice(ch * LANES, (ch + 1) * LANES)
            x_src[n, :, span] = (c * norm * ffn_gain[:, span]).astype(BF16)
        for x in near_first:
            send(x_src.at[n], x_in.at[n, my_x], 8 + n, place_of(x, my_y, my_z, my_c))
        x_in[n, my_x] = x_src[n]

    for load in w_loads:
        load.wait()
    for n in range(groups):
        whole_wait(x_in.at[n, pl.ds(0, nx - 1)], recv_sem.at[8 + n])
        both = mm(x_in[n].reshape(block, width), w_in[...])
        hidden = jnp.zeros((block, LANES), F32)
        for e in range(2):
            gate = both[:, e * LANES : (e + 1) * LANES]
            up = both[:, (2 + e) * LANES : (3 + e) * LANES]
            hidden = hidden + silu(gate) * up * masks[e, n * block : (n + 1) * block]
        h_src[n] = hidden.astype(BF16)
        for x in xs:
            send(h_src.at[n], h_in.at[n, my_x], 10 + n, place_of(x, my_y, my_z, my_c))
        h_in[n, my_x] = h_src[n]

    back_row = iota((block * x_chunks, block * x_chunks), 0)
    back_col = iota((block * x_chunks, block * x_chunks), 1)
    row_y = (back_row % msg) // x_chunks
    slot = jnp.bitwise_and(back_col, 15)
    flatten = (
        (back_row // msg == jnp.right_shift(slot, 1))
        & (row_y == SRC * (back_col // (16 * x_chunks)) + jnp.bitwise_and(slot, 1))
        & (back_row % x_chunks == jnp.right_shift(back_col, 4) % x_chunks)
    )
    flatten = flatten.astype(BF16)
    whole_wait(w_down.at[pl.ds(0, nx - 1)], recv_sem.at[15])
    for n in range(groups):
        whole_wait(h_in.at[n, pl.ds(0, nx - 1)], recv_sem.at[10 + n])
        total = jnp.zeros((block, x_width), F32)
        for x in range(nx):
            h = h_in[n, x].astype(F32)
            for e in range(2):
                chosen = (h * masks[e, n * block : (n + 1) * block]).astype(BF16)
                total = total + mm(chosen, w_down[x, e])
        total = total.astype(BF16)
        tiles = [
            total[x * 16 : (x + 1) * 16, ch * LANES : (ch + 1) * LANES]
            for x in range(nx)
            for ch in range(x_chunks)
        ]
        turned = mm(flatten, jnp.concatenate(tiles, axis=0)).astype(BF16)
        m6_src[n * 8 : (n + 1) * 8] = turned.reshape(8, ny, 4, LANES)
        for i in range(n * 4, (n + 1) * 4):
            for c in (my_c, other):
                for dy in Y_ORDER:
                    y = lax.rem(my_y + dy, ny)
                    src = m6_src.at[i * 2 + c, y]
                    if order[i] or dy or c is other:
                        send(src, m6_in.at[ep], 12, place_of(my_x, y, z_from[i], c))
                    else:
                        m6_in[ep] = m6_src[i * 2 + my_c, my_y]

    whole_wait(k_in, recv_sem.at[14])
    whole_wait(m6_in.at[pl.ds(0, owners - 1)], recv_sem.at[12])
    rows = m6_in[...].reshape(back, LANES)
    mixed = mm(weigh[0], rows) + mm(weigh[1], rows)
    mixed = mixed + k_in[...].reshape(x_chunks * PAD, LANES).astype(F32)
    for i in range(x_chunks):
        out[:, i * LANES : (i + 1) * LANES] = mixed[i * PAD : i * PAD + count].astype(BF16)

    for copy in sent:
        copy.wait_send()
    for n, copy in enumerate(k_copies):

        @pl.when(half != n)
        def _():
            copy.wait_send()


def shards(
    nx,
    ny,
    nzc,
    residual_in,
    new_query,
    new_keys,
    new_values,
    out_gate,
    beta_logit,
    decay_logit,
    decay_base,
    decay_bias,
    norm_gain,
    state_store,
    state_scale,
    arrival,
    out_weight,
    ffn_gain,
    expert_gate_weight,
    expert_up_weight,
    expert_down_weight,
    route_ids,
    route_weight,
):
    count, width = residual_in.shape
    key_heads = new_query.shape[1] // LANES
    heads = 2 * key_heads
    top = route_ids.shape[1]
    chunks = width // LANES
    y_chunks = chunks // ny
    x_chunks = chunks // nx
    owners = ny * nzc
    cols = nzc // 2 * 16
    groups = nzc // 8
    block = nx * 16
    stage_tiles = 2 * key_heads + 2 * heads + chunks
    vmem = pl.BlockSpec(memory_space=pltpu.VMEM)
    hbm = pl.BlockSpec(memory_space=pltpu.HBM)
    small_operands = (
        residual_in,
        new_query,
        new_keys,
        new_values,
        out_gate,
        beta_logit,
        decay_logit,
        decay_base[None, :],
        decay_bias[None, :],
        norm_gain[None, :],
        state_scale,
        arrival,
        ffn_gain[None, :],
        route_ids,
        route_weight,
    )
    scratch = [
        (pltpu.SMEM if a is arrival else pltpu.VMEM)(a.shape, a.dtype) for a in small_operands
    ] + [
        pltpu.VMEM((PAD, stage_tiles * LANES), F32),
        pltpu.VMEM((4, PAD, LANES), F32),
        pltpu.VMEM(state_store.shape, BF16),
        pltpu.VMEM((width, 4 * LANES), BF16),
        pltpu.VMEM((nx, 2, LANES, width // nx), BF16),
        pltpu.VMEM((cols, heads * LANES), BF16),
        pltpu.VMEM((PAD, LANES), F32),
        pltpu.VMEM((ny, PAD, LANES), F32),
        pltpu.VMEM((ny, y_chunks * PAD, LANES), BF16),
        pltpu.VMEM((ny, y_chunks * PAD, LANES), BF16),
        pltpu.VMEM((PAD, LANES), F32),
        pltpu.VMEM((nzc, PAD, LANES), F32),
        pltpu.VMEM((heads * PAD, LANES), BF16),
        pltpu.VMEM((heads * count, LANES), BF16),
        pltpu.VMEM((2 * ny, heads * count, LANES), BF16),
        pltpu.VMEM((2 * ny, heads * PAD, LANES), BF16),
        pltpu.VMEM((2, nx, ROWS, cols), F32),
        pltpu.VMEM((2 * nx, ROWS, cols), F32),
        pltpu.VMEM((SRC, y_chunks * PAD, LANES), BF16),
        pltpu.VMEM((SRC, y_chunks * PAD, LANES), BF16),
        pltpu.VMEM((owners * 4, y_chunks * ROWS), BF16),
        pltpu.VMEM((2, x_chunks * PAD, owners * 4), BF16),
        pltpu.VMEM((2, groups * block, LANES), F32),
        pltpu.VMEM((owners, 4, LANES), BF16),
        pltpu.VMEM((nzc, ny, 4, LANES), BF16),
        pltpu.VMEM((groups, 16, width), BF16),
        pltpu.VMEM((groups, nx, 16, width), BF16),
        pltpu.VMEM((groups, block, LANES), BF16),
        pltpu.VMEM((groups, nx, block, LANES), BF16),
        pltpu.VMEM((nzc, ny, 4, LANES), BF16),
        pltpu.VMEM((owners, 4, LANES), BF16),
        pltpu.SemaphoreType.DMA((len(small_operands),)),
        pltpu.SemaphoreType.DMA((8,)),
        pltpu.SemaphoreType.DMA((17,)),
        pltpu.SemaphoreType.DMA((17,)),
    ]
    return pl.pallas_call(
        functools.partial(kernel, nx, ny, nzc, top),
        out_shape=jax.ShapeDtypeStruct((count, width // nx), BF16),
        in_specs=[hbm] * (len(small_operands) + 5),
        out_specs=vmem,
        scratch_shapes=scratch,
        compiler_params=pltpu.CompilerParams(
            collective_id=0, has_side_effects=True, vmem_limit_bytes=60 * 1024 * 1024
        ),
        name="decode_layer",
    )(
        *small_operands,
        out_weight.T,
        state_store,
        expert_gate_weight,
        expert_up_weight,
        expert_down_weight,
    )


def solution(mesh):
    nx = mesh.shape["tp"]
    ny = SRC * nx
    nzc = mesh.shape["ep"] // ny
    return jax.shard_map(
        functools.partial(shards, nx, ny, nzc),
        mesh=mesh,
        in_specs=(
            P("ep", None),
            P("ep", "tp"),
            P("ep", "tp"),
            P("ep", "tp"),
            P("ep", "tp"),
            P("ep", "tp"),
            P("ep", "tp"),
            P("tp"),
            P("tp"),
            P(),
            P("ep", "tp", None, None),
            P("ep", "tp"),
            P("ep"),
            P("tp", "ep"),
            P(),
            P("ep", None, "tp"),
            P("ep", None, "tp"),
            P("ep", "tp", None),
            P("ep", None),
            P("ep", None),
        ),
        out_specs=P("ep", "tp"),
        check_vma=False,
    )
```

```python
import functools
import math

import jax
import jax.numpy as jnp
from jax import lax
from jax.experimental import pallas as pl
from jax.experimental.pallas import tpu as pltpu
from jax.sharding import PartitionSpec as P

MESH = pl.DeviceIdType.MESH
F32 = jnp.float32
BF16 = jnp.bfloat16
LANES = 128
PAD = 8
SRC = 2
Z_ORDER = (0, 1, 7, 2, 6, 3, 5, 4)
GROUP_Z = 2
GROUP_ORDER = (0, 1, 2, 3)
Y_ORDER = (4, 3, 5, 2, 6, 1, 7, 0)
ROWS = SRC * PAD
NT = (((1,), (1,)), ((), ()))
EXACT = lax.Precision.HIGHEST


def mm(a, b, dims=(((1,), (0,)), ((), ())), precision=None):
    return lax.dot_general(a, b, dims, preferred_element_type=F32, precision=precision)


def iota(shape, axis):
    return lax.broadcasted_iota(jnp.int32, shape, axis)


def silu(v):
    return v * jax.nn.sigmoid(v)


def whole_wait(ref, sem):
    pltpu.make_async_copy(ref, ref, sem).wait()


def kernel(
    nx,
    ny,
    nzc,
    top,
    residual_hbm,
    query_hbm,
    keys_hbm,
    values_hbm,
    out_gate_hbm,
    beta_logit_hbm,
    decay_logit_hbm,
    decay_base_hbm,
    decay_bias_hbm,
    norm_gain_hbm,
    state_scale_hbm,
    arrival_hbm,
    ffn_gain_hbm,
    route_ids_hbm,
    route_weight_hbm,
    out_weight_hbm,
    state_hbm,
    gate_hbm,
    up_hbm,
    down_hbm,
    out,
    residual,
    query,
    keys,
    values,
    out_gate,
    beta_logit,
    decay_logit,
    decay_base,
    decay_bias,
    norm_gain,
    state_scale,
    arrival,
    ffn_gain,
    route_ids,
    route_weight,
    stage,
    small,
    state,
    w_in,
    w_down,
    w_out,
    r0_src,
    r0_in,
    b_src,
    b_in,
    r1_src,
    r1_in,
    g_pad,
    g_src,
    g_in,
    g_all,
    p_src,
    p_in,
    k_src,
    k_in,
    place,
    weigh,
    masks,
    m3_src,
    m3_in,
    x_src,
    x_in,
    h_src,
    h_in,
    m6_src,
    m6_in,
    small_sem,
    load_sem,
    send_sem,
    recv_sem,
):
    count, width = residual_hbm.shape
    chunks = width // LANES
    y_chunks = chunks // ny
    x_chunks = chunks // nx
    key_heads = query_hbm.shape[1] // LANES
    heads = 2 * key_heads
    nz = nzc // 2
    cols = nz * 16
    per_x = GROUP_Z * 2 * SRC
    flat = per_x * chunks
    owners = ny * nzc
    back = owners * 4
    groups = nz // GROUP_Z
    g_zc = 2 * GROUP_Z
    block = nx * per_x

    ep = lax.axis_index("ep")
    my_x = lax.axis_index("tp")
    my_y = ep // nzc
    my_zc = lax.rem(ep, nzc)
    my_z = my_zc // 2
    my_c = lax.rem(my_zc, 2)
    other = 1 - my_c

    def place_of(x, y, z, c):
        return (y * nzc + z * 2 + c, x)

    def at_zc(zc):
        return (my_y * nzc + zc, my_x)

    xs = [lax.rem(my_x + d, nx) for d in range(1, nx)]
    near_first = xs[0:1] + xs[2:] + xs[1:2]
    ys = [lax.rem(my_y + d, ny) for d in range(1, ny)]
    zs = [lax.rem(my_z + d, nz) for d in range(1, nz)]
    zcs = [lax.rem(my_zc + d, nzc) for d in range(1, nzc)]
    sibling = place_of(my_x, my_y, my_z, other)

    order = Z_ORDER
    z_from = [lax.rem(my_z + d, nz) for d in order]
    z_to = [lax.rem(my_z + nz - d, nz) for d in order]

    sent = []

    def remote(src, dst, hop, target):
        return pltpu.make_async_remote_copy(
            src_ref=src,
            dst_ref=dst,
            send_sem=send_sem.at[hop],
            recv_sem=recv_sem.at[hop],
            device_id=target,
            device_id_type=MESH,
        )

    def send(src, dst, hop, target):
        copy = remote(src, dst, hop, target)
        copy.start()
        sent.append(copy)

    own_cols = pl.ds(pl.multiple_of(my_z * 16, 16), 16)
    smalls = [
        pltpu.make_async_copy(src, dst, small_sem.at[n])
        for n, (src, dst) in enumerate(
            (
                (route_ids_hbm, route_ids),
                (route_weight_hbm, route_weight),
                (residual_hbm, residual),
                (query_hbm, query),
                (keys_hbm, keys),
                (values_hbm, values),
                (out_gate_hbm, out_gate),
                (beta_logit_hbm, beta_logit),
                (decay_logit_hbm, decay_logit),
                (decay_base_hbm, decay_base),
                (decay_bias_hbm, decay_bias),
                (norm_gain_hbm, norm_gain),
                (state_scale_hbm, state_scale),
                (arrival_hbm, arrival),
                (ffn_gain_hbm, ffn_gain),
            )
        )
    ]
    for load in smalls:
        load.start()
    state_load = pltpu.make_async_copy(state_hbm, state, load_sem.at[0])
    state_load.start()
    w_own = pltpu.make_async_copy(out_weight_hbm, w_out.at[own_cols, :], load_sem.at[1])
    w_own.start()

    barrier = pltpu.get_barrier_semaphore()
    peers = [
        place_of(my_x, lax.rem(my_y + d, ny), my_z, c) for d in Y_ORDER for c in (my_c, other) if d
    ]
    peers += [place_of(my_x, my_y, lax.rem(my_z + d, nz), my_c) for d in Y_ORDER if d]
    peers += [place_of(x, my_y, my_z, my_c) for x in xs]
    peers.append(sibling)
    for peer in peers:
        pl.semaphore_signal(barrier, inc=1, device_id=peer, device_id_type=MESH)
    pl.semaphore_wait(barrier, len(peers))

    for z in zs:
        send(out_weight_hbm, w_out.at[own_cols, :], 1, place_of(my_x, my_y, z, my_c))

    x_width = x_chunks * LANES
    for x in near_first[0:2]:
        span = pl.ds(pl.multiple_of(x * x_width, x_width), x_width)
        send(down_hbm.at[:, :, span], w_down.at[my_x], 15, place_of(x, my_y, my_z, my_c))
    far = place_of(xs[1], my_y, my_z, my_c)
    far_span = pl.ds(pl.multiple_of(xs[1] * x_width, x_width), x_width)
    send(down_hbm.at[0, :, far_span], w_down.at[my_x, 0], 15, far)

    stage[...] = jnp.zeros_like(stage)
    small[...] = jnp.zeros_like(small)
    q_at, k_at, v_at, g_at = 0, key_heads, 2 * key_heads, 2 * key_heads + heads
    r_at = g_at + heads
    for load in smalls:
        load.wait()
    for at, ref in ((q_at, query), (k_at, keys), (v_at, values), (g_at, out_gate)):
        stage[0:count, at * LANES : at * LANES + ref.shape[1]] = ref[...].astype(F32)
    small[2, 0:count, 0:heads] = decay_logit[...]
    small[3, 0:count, 0:heads] = beta_logit[...]
    rate = jnp.exp(decay_base[...])
    logit = small[2, :, 0:heads] + decay_bias[...]
    soft = jnp.maximum(logit, 0.0) + jnp.log1p(jnp.exp(-jnp.abs(logit)))
    decay = jnp.exp(-rate * soft)
    beta = jax.nn.sigmoid(small[3, :, 0:heads])
    row8 = iota((PAD, 1), 0)
    moved = jnp.zeros((PAD, heads), F32)
    for r in range(count):
        moved = jnp.where(row8 == r, state_scale[pl.ds(arrival[r], 1), :], moved)
    carry = moved * decay
    gain = norm_gain[...]
    state_load.wait()
    for g in range(key_heads):
        q = stage[:, (q_at + g) * LANES : (q_at + g + 1) * LANES]
        k = stage[:, (k_at + g) * LANES : (k_at + g + 1) * LANES]
        q = q * (lax.rsqrt(jnp.sum(q * q, axis=1, keepdims=True) + 1e-06) / math.sqrt(LANES))
        k = k * lax.rsqrt(jnp.sum(k * k, axis=1, keepdims=True) + 1e-06)
        qk = jnp.sum(q * k, axis=1, keepdims=True)
        k_hi = k.astype(BF16).astype(F32)
        q_hi = q.astype(BF16).astype(F32)
        lhs = jnp.concatenate([k_hi, k - k_hi, q_hi, q - q_hi], axis=0).astype(BF16)
        from_k = jnp.zeros((PAD, 2 * LANES), F32)
        from_q = jnp.zeros((PAD, 2 * LANES), F32)
        for r in range(count):
            row = arrival[r]
            both = jnp.concatenate([state[row, 2 * g], state[row, 2 * g + 1]], axis=1)
            got = mm(lhs, both)
            from_k = jnp.where(row8 == r, got[0:8] + got[8:16], from_k)
            from_q = jnp.where(row8 == r, got[16:24] + got[24:32], from_q)
        pair = []
        for i in range(2):
            h = 2 * g + i
            s = carry[:, h : h + 1]
            v = stage[:, (v_at + h) * LANES : (v_at + h + 1) * LANES]
            z = stage[:, (g_at + h) * LANES : (g_at + h + 1) * LANES]
            delta = beta[:, h : h + 1] * (v - s * from_k[:, i * LANES : (i + 1) * LANES])
            o = s * from_q[:, i * LANES : (i + 1) * LANES] + qk * delta
            norm = lax.rsqrt(jnp.mean(o * o, axis=1, keepdims=True) + 1e-06)
            pair.append(o * norm * gain * silu(z))
        g_pad[g * 16 : (g + 1) * 16, :] = jnp.concatenate(pair, axis=0).astype(BF16)
    row = iota((count * heads, heads * PAD), 0)
    col = iota((count * heads, heads * PAD), 1)
    filled = jnp.bitwise_and(col, 7) < count
    pack = (row == jnp.right_shift(col, 3) * count + jnp.bitwise_and(col, 7)) & filled
    g_src[...] = mm(pack.astype(BF16), g_pad[...]).astype(BF16)
    for y in ys:
        for c in (my_c, other):
            send(g_src, g_in.at[my_c * ny + my_y], 2, place_of(my_x, y, my_z, c))
    send(g_src, g_in.at[my_c * ny + my_y], 2, sibling)
    g_in[my_c * ny + my_y] = g_src[...]

    small[0, 0:count, 0:top] = (route_ids[...] + 1).astype(F32)
    small[1, 0:count, 0:top] = route_weight[...]
    r0_src[...] = pltpu.roll(small[0], my_y * top, 1).astype(BF16)
    stage[0:count, r_at * LANES : r_at * LANES + width] = residual[...].astype(F32)
    for y in range(ny):
        at = (r_at + y * y_chunks) * LANES
        tiles = [stage[:, at + i * LANES : at + (i + 1) * LANES] for i in range(y_chunks)]
        b_src[y] = jnp.concatenate(tiles, axis=0).astype(BF16)
    for y in ys:
        send(r0_src, r0_in.at[my_y], 0, place_of(my_x, y, my_z, my_c))
        send(b_src.at[y], b_in.at[my_y], 16, place_of(my_x, y, my_z, my_c))
    r0_in[my_y] = r0_src[...]
    b_in[my_y] = b_src[my_y]

    w_loads = []
    for e in range(2):
        for n, ref in ((0, gate_hbm), (2, up_hbm)):
            w_loads.append(
                pltpu.make_async_copy(
                    ref.at[e], w_in.at[:, pl.ds((n + e) * LANES, LANES)], load_sem.at[2 + n + e]
                )
            )
    own_width = pl.ds(pl.multiple_of(my_x * x_width, x_width), x_width)
    w_loads.append(
        pltpu.make_async_copy(down_hbm.at[:, :, own_width], w_down.at[my_x], load_sem.at[6])
    )
    for load in w_loads:
        load.start()

    w_own.wait()
    whole_wait(w_out.at[pl.ds(0, (nz - 1) * 16), :], recv_sem.at[1])
    row = iota((4 * heads * PAD, 4 * heads * count), 0)
    col = iota((4 * heads * PAD, 4 * heads * count), 1)
    filled = jnp.bitwise_and(row, 7) < count
    unpack = (col == jnp.right_shift(row, 3) * count + jnp.bitwise_and(row, 7)) & filled
    unpack = unpack.astype(BF16)
    whole_wait(g_in.at[pl.ds(0, 2 * ny - 1)], recv_sem.at[2])
    for n in range(0, 2 * ny, 4):
        four = mm(unpack, g_in[n : n + 4].reshape(4 * heads * count, LANES))
        g_all[n : n + 4] = four.astype(BF16).reshape(4, heads * PAD, LANES)
    first = jnp.zeros((2 * ny * 16, cols), F32)
    second = jnp.zeros((2 * ny * 16, cols), F32)
    for g in range(key_heads):
        rows = g_all[:, g * 16 : (g + 1) * 16, :].reshape(2 * ny * 16, LANES)
        first += mm(rows, w_out[:, 2 * g * LANES : (2 * g + 1) * LANES], NT)
        second += mm(rows, w_out[:, (2 * g + 1) * LANES : (2 * g + 2) * LANES], NT)
    part = first.reshape(2 * ny, 2, PAD, cols)[:, 0] + second.reshape(2 * ny, 2, PAD, cols)[:, 1]
    p_src[...] = part.reshape(2, nx, ROWS, cols)
    for x in xs:
        for c in (my_c, other):
            send(p_src.at[c, x], p_in.at[my_c * nx + my_x], 4, place_of(x, my_y, my_z, c))
    send(p_src.at[other, my_x], p_in.at[my_c * nx + my_x], 4, sibling)
    p_in[my_c * nx + my_x] = p_src[my_c, my_x]
    whole_wait(r0_in.at[pl.ds(0, ny - 1)], recv_sem.at[0])
    ids = jnp.sum(r0_in[...].astype(F32), axis=0)
    r1_src[...] = ids.astype(BF16)
    for zc in zcs:
        send(r1_src, r1_in.at[my_zc], 3, at_zc(zc))
    r1_in[my_zc] = r1_src[...]

    here = y_chunks * ROWS
    sel_row = iota((32, LANES), 0)
    pick = jnp.bitwise_and(sel_row, 15)
    source = SRC * my_x + jnp.right_shift(sel_row, 4)
    sel = ((iota((32, LANES), 1) == source * top + pick) & (pick < top)).astype(F32)
    spread = (iota((PAD, here), 0) == jnp.bitwise_and(iota((PAD, here), 1), 7)).astype(F32)
    of_source = jnp.bitwise_and(jnp.right_shift(iota((16, here), 1), 3), 1)
    wide = mm(mm(sel, ids, NT, EXACT), spread, precision=EXACT)
    owner = jnp.where(of_source == 0, wide[0:16], wide[16:32])
    owner = jnp.floor((owner - 1.0) * 0.5).astype(jnp.int32)
    owner_row = iota((owners, here), 0)
    hit = jnp.zeros((owners, here), F32)
    for j in range(top):
        hit = hit + jnp.where(owner_row == owner[j : j + 1, :], 1.0, 0.0)
    each = (iota((owners * 4, owners), 1) == jnp.right_shift(iota((owners * 4, owners), 0), 2))
    row = iota((owners * 4, here), 0)
    col = iota((owners * 4, here), 1)
    match = (jnp.bitwise_and(jnp.right_shift(row, 1), 1) == jnp.bitwise_and(jnp.right_shift(col, 3), 1)) & (
        jnp.bitwise_and(row, 1) == jnp.right_shift(col, 4)
    )
    place[...] = jnp.where(match, mm(each.astype(BF16), hit.astype(BF16)), 0.0).astype(BF16)

    own_ids = small[0]
    own_weight = small[1]
    lane = iota((PAD, LANES), 1)
    share = jnp.zeros((PAD, owners), F32)
    for j in range(top):
        named = jnp.floor((own_ids[:, j : j + 1] - 1.0) * 0.5).astype(jnp.int32)
        share = share + jnp.where(lane == named, own_weight[:, j : j + 1], 0.0)
    hi = share.astype(BF16).astype(F32)
    open_up = iota((owners, back), 0) == jnp.right_shift(iota((owners, back), 1), 2)
    both = mm(jnp.concatenate([hi, share - hi], axis=0).astype(BF16), open_up.astype(BF16))
    row = iota((x_chunks * PAD, back), 0)
    kept = jnp.right_shift(row, 3) == jnp.bitwise_and(iota((x_chunks * PAD, back), 1), 3)
    for n in range(2):
        tall = jnp.concatenate([both[n * PAD : (n + 1) * PAD]] * x_chunks, axis=0)
        weigh[n] = jnp.where(kept, tall, 0.0).astype(BF16)

    mix_row = iota((2 * cols, 2 * cols), 0)
    mix_col = iota((2 * cols, 2 * cols), 1)
    mix = (
        (mix_row // cols == jnp.bitwise_and(jnp.right_shift(mix_col, 4), 1))
        & (
            jnp.right_shift(jnp.bitwise_and(mix_row, cols - 1), 4)
            == jnp.right_shift(mix_col, 5)
        )
        & (jnp.bitwise_and(mix_row, 15) == jnp.bitwise_and(mix_col, 15))
    )
    mix = mix.astype(BF16)

    whole_wait(b_in.at[pl.ds(0, ny - 1)], recv_sem.at[16])
    whole_wait(p_in.at[pl.ds(0, 2 * nx - 1)], recv_sem.at[4])
    attn = []
    for c in range(2):
        total = p_in[c * nx]
        for x in range(1, nx):
            total = total + p_in[c * nx + x]
        attn.append(total.astype(BF16))
    attn = mm(jnp.concatenate(attn, axis=1), mix)
    base_rows = [b_in[SRC * my_x + s].astype(F32) for s in range(SRC)]
    parts = []
    for i in range(y_chunks):
        base = jnp.concatenate([rows[i * PAD : (i + 1) * PAD] for rows in base_rows], axis=0)
        parts.append(base + attn[:, i * LANES : (i + 1) * LANES])
    carried = jnp.concatenate(parts, axis=0).astype(BF16)

    m3_src[...] = mm(place[...], carried).astype(BF16).reshape(owners, 4, LANES)
    for i, z in enumerate(z_to):
        for c in (my_c, other):
            for dy in Y_ORDER:
                y = lax.rem(my_y + dy, ny)
                to = place_of(my_x, y, z, c)
                src = m3_src.at[to[0]]
                dst = m3_in.at[i * 2 + my_c, my_y]
                if order[i] or dy or c is other:
                    send(src, dst, 20 + i // GROUP_Z, to)
                else:
                    pltpu.make_async_copy(src, dst, recv_sem.at[20 + i // GROUP_Z]).start()

    half = my_y - SRC * my_x
    wide = carried.astype(F32)
    to_x = my_y // SRC
    k_dst = k_in.at[my_y - SRC * to_x]
    k_copies = []
    for n in range(SRC):
        rows = [wide[i * ROWS + n * PAD : i * ROWS + (n + 1) * PAD] for i in range(y_chunks)]
        k_src[n] = jnp.concatenate(rows, axis=0).astype(BF16)
        away = remote(k_src.at[n], k_dst, 14, place_of(to_x, SRC * my_x + n, my_z, my_c))
        keep = pltpu.make_async_copy(k_src.at[n], k_dst, recv_sem.at[14])
        k_copies.append(away)

        @pl.when(half == n)
        def _():
            keep.start()

        @pl.when(half != n)
        def _():
            away.start()

    send(down_hbm.at[1, :, far_span], w_down.at[my_x, 1], 15, far)

    whole_wait(r1_in.at[pl.ds(0, nzc - 1)], recv_sem.at[3])
    slot = iota((groups * block, nzc), 0)
    slot_i = (slot // block) * GROUP_Z + jnp.bitwise_and(
        jnp.right_shift(slot, 2), GROUP_Z - 1
    )
    slot_z = jnp.zeros_like(slot)
    for i, z in enumerate(z_from):
        slot_z = jnp.where(slot_i == i, z, slot_z)
    slot_zc = slot_z * 2 + jnp.bitwise_and(jnp.right_shift(slot, 1), 1)
    of_zc = (slot_zc == iota((groups * block, nzc), 1)).astype(BF16)
    slot = iota((groups * block, LANES), 0)
    slot_x = jnp.bitwise_and(slot, block - 1) // per_x
    slot_y = SRC * slot_x + jnp.bitwise_and(slot, 1)
    lane = iota((groups * block, LANES), 1)
    of_y = (lane >= slot_y * top) & (lane < slot_y * top + top)
    arrived = r1_in[...].astype(F32)
    for e in range(2):
        named = (2 * ep + 1 + e).astype(F32)
        found = jnp.sum(jnp.where(arrived == named, 1.0, 0.0), axis=1).astype(BF16)
        found = jnp.where(of_y, mm(of_zc, found), 0.0)
        masks[e] = jnp.broadcast_to(
            jnp.sum(found, axis=1, keepdims=True), (groups * block, LANES)
        )

    turn_row = iota((flat, flat), 0)
    turn_col = iota((flat, flat), 1)
    turn_ch = turn_row // per_x
    turn_slot = turn_row % per_x
    unflat = turn_col == (
        (turn_slot // 2) * (ny * 4)
        + (turn_ch // y_chunks) * 4
        + jnp.bitwise_and(turn_slot, 1) * y_chunks
        + turn_ch % y_chunks
    )
    unflat = unflat.astype(BF16)
    for n in GROUP_ORDER:
        whole_wait(m3_in.at[pl.ds(n * g_zc, g_zc)], recv_sem.at[20 + n])
        turned = mm(unflat, m3_in[n * g_zc : (n + 1) * g_zc].reshape(flat, LANES))
        squares = jnp.zeros((per_x, LANES), F32)
        for ch in range(chunks):
            c = turned[ch * per_x : (ch + 1) * per_x]
            squares = squares + c * c
        norm = lax.rsqrt(jnp.sum(squares, axis=1, keepdims=True) / width + 1e-06)
        for ch in range(chunks):
            c = turned[ch * per_x : (ch + 1) * per_x]
            span = slice(ch * LANES, (ch + 1) * LANES)
            x_src[n, :, span] = (c * norm * ffn_gain[:, span]).astype(BF16)
        for x in near_first:
            send(x_src.at[n], x_in.at[n, my_x], 24 + n, place_of(x, my_y, my_z, my_c))
        x_in[n, my_x] = x_src[n]

    back_row = iota((block * x_chunks, block * x_chunks), 0)
    back_col = iota((block * x_chunks, block * x_chunks), 1)
    each_zc = ny * x_chunks
    row_y = (back_row % each_zc) // x_chunks
    slot = back_col % per_x
    flatten = (
        (back_row // each_zc == jnp.right_shift(slot, 1))
        & (row_y == SRC * (back_col // (per_x * x_chunks)) + jnp.bitwise_and(slot, 1))
        & (back_row % x_chunks == (back_col // per_x) % x_chunks)
    )
    flatten = flatten.astype(BF16)
    for load in w_loads:
        load.wait()

    def hidden_of(n):
        whole_wait(x_in.at[n, pl.ds(0, nx - 1)], recv_sem.at[24 + n])
        both = mm(x_in[n].reshape(block, width), w_in[...])
        hidden = jnp.zeros((block, LANES), F32)
        for e in range(2):
            gate = both[:, e * LANES : (e + 1) * LANES]
            up = both[:, (2 + e) * LANES : (3 + e) * LANES]
            hidden = hidden + silu(gate) * up * masks[e, n * block : (n + 1) * block]
        h_src[n] = hidden.astype(BF16)
        for x in near_first:
            send(h_src.at[n], h_in.at[n, my_x], 28 + n, place_of(x, my_y, my_z, my_c))
        h_in[n, my_x] = h_src[n]

    def output_of(n):
        whole_wait(h_in.at[n, pl.ds(0, nx - 1)], recv_sem.at[28 + n])
        parts = []
        for x in range(nx):
            h = h_in[n, x].astype(F32)
            for e in range(2):
                parts.append(h * masks[e, n * block : (n + 1) * block])
        total = mm(
            jnp.concatenate(parts, axis=1).astype(BF16),
            w_down[...].reshape(nx * 2 * LANES, x_width),
        )
        tiles = [
            total[x * per_x : (x + 1) * per_x, ch * LANES : (ch + 1) * LANES]
            for x in range(nx)
            for ch in range(x_chunks)
        ]
        turned = mm(flatten, jnp.concatenate(tiles, axis=0).astype(BF16)).astype(BF16)
        m6_src[n * g_zc : (n + 1) * g_zc] = turned.reshape(g_zc, ny, 4, LANES)
        for i in range(n * GROUP_Z, (n + 1) * GROUP_Z):
            for c in (my_c, other):
                for dy in Y_ORDER:
                    y = lax.rem(my_y + dy, ny)
                    src = m6_src.at[i * 2 + c, y]
                    if order[i] or dy or c is other:
                        send(src, m6_in.at[ep], 12, place_of(my_x, y, z_from[i], c))
                    else:
                        m6_in[ep] = m6_src[i * 2 + my_c, my_y]

    lag = groups
    for k, n in enumerate(GROUP_ORDER):
        hidden_of(n)
        if k == lag - 1:
            whole_wait(w_down.at[pl.ds(0, nx - 1)], recv_sem.at[15])
        if k >= lag:
            output_of(GROUP_ORDER[k - lag])
    for n in GROUP_ORDER[groups - lag :]:
        output_of(n)

    whole_wait(k_in, recv_sem.at[14])
    whole_wait(m6_in.at[pl.ds(0, owners - 1)], recv_sem.at[12])
    rows = m6_in[...].reshape(back, LANES)
    mixed = mm(weigh[0], rows) + mm(weigh[1], rows)
    mixed = mixed + k_in[...].reshape(x_chunks * PAD, LANES).astype(F32)
    for i in range(x_chunks):
        out[:, i * LANES : (i + 1) * LANES] = mixed[i * PAD : i * PAD + count].astype(BF16)

    for copy in sent:
        copy.wait_send()
    for n, copy in enumerate(k_copies):

        @pl.when(half != n)
        def _():
            copy.wait_send()


def shards(
    nx,
    ny,
    nzc,
    residual_in,
    new_query,
    new_keys,
    new_values,
    out_gate,
    beta_logit,
    decay_logit,
    decay_base,
    decay_bias,
    norm_gain,
    state_store,
    state_scale,
    arrival,
    out_weight,
    ffn_gain,
    expert_gate_weight,
    expert_up_weight,
    expert_down_weight,
    route_ids,
    route_weight,
):
    count, width = residual_in.shape
    key_heads = new_query.shape[1] // LANES
    heads = 2 * key_heads
    top = route_ids.shape[1]
    chunks = width // LANES
    y_chunks = chunks // ny
    x_chunks = chunks // nx
    owners = ny * nzc
    cols = nzc // 2 * 16
    groups = nzc // 2 // GROUP_Z
    per_x = GROUP_Z * 2 * SRC
    block = nx * per_x
    stage_tiles = 2 * key_heads + 2 * heads + chunks
    vmem = pl.BlockSpec(memory_space=pltpu.VMEM)
    hbm = pl.BlockSpec(memory_space=pltpu.HBM)
    small_operands = (
        residual_in,
        new_query,
        new_keys,
        new_values,
        out_gate,
        beta_logit,
        decay_logit,
        decay_base[None, :],
        decay_bias[None, :],
        norm_gain[None, :],
        state_scale,
        arrival,
        ffn_gain[None, :],
        route_ids,
        route_weight,
    )
    scratch = [
        (pltpu.SMEM if a is arrival else pltpu.VMEM)(a.shape, a.dtype) for a in small_operands
    ] + [
        pltpu.VMEM((PAD, stage_tiles * LANES), F32),
        pltpu.VMEM((4, PAD, LANES), F32),
        pltpu.VMEM(state_store.shape, BF16),
        pltpu.VMEM((width, 4 * LANES), BF16),
        pltpu.VMEM((nx, 2, LANES, width // nx), BF16),
        pltpu.VMEM((cols, heads * LANES), BF16),
        pltpu.VMEM((PAD, LANES), BF16),
        pltpu.VMEM((ny, PAD, LANES), BF16),
        pltpu.VMEM((ny, y_chunks * PAD, LANES), BF16),
        pltpu.VMEM((ny, y_chunks * PAD, LANES), BF16),
        pltpu.VMEM((PAD, LANES), BF16),
        pltpu.VMEM((nzc, PAD, LANES), BF16),
        pltpu.VMEM((heads * PAD, LANES), BF16),
        pltpu.VMEM((heads * count, LANES), BF16),
        pltpu.VMEM((2 * ny, heads * count, LANES), BF16),
        pltpu.VMEM((2 * ny, heads * PAD, LANES), BF16),
        pltpu.VMEM((2, nx, ROWS, cols), F32),
        pltpu.VMEM((2 * nx, ROWS, cols), F32),
        pltpu.VMEM((SRC, y_chunks * PAD, LANES), BF16),
        pltpu.VMEM((SRC, y_chunks * PAD, LANES), BF16),
        pltpu.VMEM((owners * 4, y_chunks * ROWS), BF16),
        pltpu.VMEM((2, x_chunks * PAD, owners * 4), BF16),
        pltpu.VMEM((2, groups * block, LANES), F32),
        pltpu.VMEM((owners, 4, LANES), BF16),
        pltpu.VMEM((nzc, ny, 4, LANES), BF16),
        pltpu.VMEM((groups, per_x, width), BF16),
        pltpu.VMEM((groups, nx, per_x, width), BF16),
        pltpu.VMEM((groups, block, LANES), BF16),
        pltpu.VMEM((groups, nx, block, LANES), BF16),
        pltpu.VMEM((nzc, ny, 4, LANES), BF16),
        pltpu.VMEM((owners, 4, LANES), BF16),
        pltpu.SemaphoreType.DMA((len(small_operands),)),
        pltpu.SemaphoreType.DMA((8,)),
        pltpu.SemaphoreType.DMA((32,)),
        pltpu.SemaphoreType.DMA((32,)),
    ]
    return pl.pallas_call(
        functools.partial(kernel, nx, ny, nzc, top),
        out_shape=pltpu.VMEM((count, width // nx), BF16),
        in_specs=[hbm] * (len(small_operands) + 5),
        out_specs=vmem,
        scratch_shapes=scratch,
        compiler_params=pltpu.CompilerParams(
            collective_id=0, has_side_effects=True, vmem_limit_bytes=60 * 1024 * 1024
        ),
        name="decode_layer",
    )(
        *small_operands,
        out_weight.T,
        state_store,
        expert_gate_weight,
        expert_up_weight,
        expert_down_weight,
    )


def solution(mesh):
    nx = mesh.shape["tp"]
    ny = SRC * nx
    nzc = mesh.shape["ep"] // ny
    return jax.shard_map(
        functools.partial(shards, nx, ny, nzc),
        mesh=mesh,
        in_specs=(
            P("ep", None),
            P("ep", "tp"),
            P("ep", "tp"),
            P("ep", "tp"),
            P("ep", "tp"),
            P("ep", "tp"),
            P("ep", "tp"),
            P("tp"),
            P("tp"),
            P(),
            P("ep", "tp", None, None),
            P("ep", "tp"),
            P("ep"),
            P("tp", "ep"),
            P(),
            P("ep", None, "tp"),
            P("ep", None, "tp"),
            P("ep", "tp", None),
            P("ep", None),
            P("ep", None),
        ),
        out_specs=P("ep", "tp"),
        check_vma=False,
    )
```

```python
import functools
import math

import jax
import jax.numpy as jnp
from jax import lax
from jax.experimental import pallas as pl
from jax.experimental.pallas import tpu as pltpu
from jax.sharding import PartitionSpec as P

MESH = pl.DeviceIdType.MESH
F32 = jnp.float32
BF16 = jnp.bfloat16
LANES = 128
PAD = 8
SRC = 2
Z_ORDER = (0, 1, 7, 2, 6, 3, 5, 4)
GROUP_Z = 2
GROUP_ORDER = (0, 1, 2, 3)
Y_ORDER = (4, 3, 5, 2, 6, 1, 7, 0)
ROWS = SRC * PAD
NT = (((1,), (1,)), ((), ()))
EXACT = lax.Precision.HIGHEST


def mm(a, b, dims=(((1,), (0,)), ((), ())), precision=None):
    return lax.dot_general(a, b, dims, preferred_element_type=F32, precision=precision)


def iota(shape, axis):
    return lax.broadcasted_iota(jnp.int32, shape, axis)


def silu(v):
    return v * jax.nn.sigmoid(v)


def whole_wait(ref, sem):
    pltpu.make_async_copy(ref, ref, sem).wait()


def kernel(
    nx,
    ny,
    nzc,
    top,
    residual_hbm,
    query_hbm,
    keys_hbm,
    values_hbm,
    out_gate_hbm,
    beta_logit_hbm,
    decay_logit_hbm,
    decay_base_hbm,
    decay_bias_hbm,
    norm_gain_hbm,
    state_scale_hbm,
    arrival_hbm,
    ffn_gain_hbm,
    route_ids_hbm,
    route_weight_hbm,
    out_weight_hbm,
    state_hbm,
    gate_hbm,
    up_hbm,
    down_hbm,
    out,
    residual,
    query,
    keys,
    values,
    out_gate,
    beta_logit,
    decay_logit,
    decay_base,
    decay_bias,
    norm_gain,
    state_scale,
    arrival,
    ffn_gain,
    route_ids,
    route_weight,
    stage,
    small,
    state,
    w_in,
    w_down,
    w_out,
    r0_src,
    r0_in,
    b_src,
    b_in,
    r1_src,
    r1_in,
    g_pad,
    g_src,
    g_in,
    g_all,
    p_src,
    p_in,
    k_src,
    k_in,
    place,
    weigh,
    masks,
    m3_src,
    m3_in,
    x_src,
    x_in,
    h_src,
    h_in,
    m6_src,
    m6_in,
    small_sem,
    load_sem,
    send_sem,
    recv_sem,
):
    count, width = residual_hbm.shape
    chunks = width // LANES
    y_chunks = chunks // ny
    x_chunks = chunks // nx
    key_heads = query_hbm.shape[1] // LANES
    heads = 2 * key_heads
    nz = nzc // 2
    cols = nz * 16
    per_x = GROUP_Z * 2 * SRC
    flat = per_x * chunks
    owners = ny * nzc
    back = owners * 4
    groups = nz // GROUP_Z
    g_zc = 2 * GROUP_Z
    block = nx * per_x

    ep = lax.axis_index("ep")
    my_x = lax.axis_index("tp")
    my_y = ep // nzc
    my_zc = lax.rem(ep, nzc)
    my_z = my_zc // 2
    my_c = lax.rem(my_zc, 2)
    other = 1 - my_c

    def place_of(x, y, z, c):
        return (y * nzc + z * 2 + c, x)

    def at_zc(zc):
        return (my_y * nzc + zc, my_x)

    xs = [lax.rem(my_x + d, nx) for d in range(1, nx)]
    near_first = xs[0:1] + xs[2:] + xs[1:2]
    far_first = xs[1:2] + xs[0:1] + xs[2:]
    ys = [lax.rem(my_y + d, ny) for d in Y_ORDER if d]
    zs = [lax.rem(my_z + d, nz) for d in Y_ORDER if d]
    zcs = [lax.rem(my_zc + d, nzc) for d in range(1, nzc)]
    sibling = place_of(my_x, my_y, my_z, other)

    order = Z_ORDER
    z_from = [lax.rem(my_z + d, nz) for d in order]
    z_to = [lax.rem(my_z + nz - d, nz) for d in order]

    sent = []

    def remote(src, dst, hop, target):
        return pltpu.make_async_remote_copy(
            src_ref=src,
            dst_ref=dst,
            send_sem=send_sem.at[hop],
            recv_sem=recv_sem.at[hop],
            device_id=target,
            device_id_type=MESH,
        )

    def send(src, dst, hop, target):
        copy = remote(src, dst, hop, target)
        copy.start()
        sent.append(copy)

    own_cols = pl.ds(pl.multiple_of(my_z * 16, 16), 16)
    smalls = [
        pltpu.make_async_copy(src, dst, small_sem.at[n])
        for n, (src, dst) in enumerate(
            (
                (route_ids_hbm, route_ids),
                (route_weight_hbm, route_weight),
                (residual_hbm, residual),
                (query_hbm, query),
                (keys_hbm, keys),
                (values_hbm, values),
                (out_gate_hbm, out_gate),
                (beta_logit_hbm, beta_logit),
                (decay_logit_hbm, decay_logit),
                (decay_base_hbm, decay_base),
                (decay_bias_hbm, decay_bias),
                (norm_gain_hbm, norm_gain),
                (state_scale_hbm, state_scale),
                (arrival_hbm, arrival),
                (ffn_gain_hbm, ffn_gain),
            )
        )
    ]
    for load in smalls:
        load.start()
    state_load = pltpu.make_async_copy(state_hbm, state, load_sem.at[0])
    state_load.start()
    w_own = pltpu.make_async_copy(out_weight_hbm, w_out.at[own_cols, :], load_sem.at[1])
    w_own.start()

    barrier = pltpu.get_barrier_semaphore()
    peers = [
        place_of(my_x, lax.rem(my_y + d, ny), my_z, c) for d in Y_ORDER for c in (my_c, other) if d
    ]
    peers += [place_of(my_x, my_y, lax.rem(my_z + d, nz), my_c) for d in Y_ORDER if d]
    peers += [place_of(x, my_y, my_z, my_c) for x in xs]
    peers.append(sibling)
    for peer in peers:
        pl.semaphore_signal(barrier, inc=1, device_id=peer, device_id_type=MESH)
    pl.semaphore_wait(barrier, len(peers))

    for z in zs:
        send(out_weight_hbm, w_out.at[own_cols, :], 1, place_of(my_x, my_y, z, my_c))

    x_width = x_chunks * LANES
    for x in near_first[0:2]:
        span = pl.ds(pl.multiple_of(x * x_width, x_width), x_width)
        send(down_hbm.at[:, :, span], w_down.at[my_x], 15, place_of(x, my_y, my_z, my_c))
    far = place_of(xs[1], my_y, my_z, my_c)
    far_span = pl.ds(pl.multiple_of(xs[1] * x_width, x_width), x_width)
    send(down_hbm.at[0, :, far_span], w_down.at[my_x, 0], 15, far)

    stage[...] = jnp.zeros_like(stage)
    small[...] = jnp.zeros_like(small)
    q_at, k_at, v_at, g_at = 0, key_heads, 2 * key_heads, 2 * key_heads + heads
    r_at = g_at + heads
    for load in smalls:
        load.wait()
    for at, ref in ((q_at, query), (k_at, keys), (v_at, values), (g_at, out_gate)):
        stage[0:count, at * LANES : at * LANES + ref.shape[1]] = ref[...].astype(F32)
    small[2, 0:count, 0:heads] = decay_logit[...]
    small[3, 0:count, 0:heads] = beta_logit[...]
    rate = jnp.exp(decay_base[...])
    logit = small[2, :, 0:heads] + decay_bias[...]
    soft = jnp.maximum(logit, 0.0) + jnp.log1p(jnp.exp(-jnp.abs(logit)))
    decay = jnp.exp(-rate * soft)
    beta = jax.nn.sigmoid(small[3, :, 0:heads])
    row8 = iota((PAD, 1), 0)
    moved = jnp.zeros((PAD, heads), F32)
    for r in range(count):
        moved = jnp.where(row8 == r, state_scale[pl.ds(arrival[r], 1), :], moved)
    carry = moved * decay
    gain = norm_gain[...]
    state_load.wait()
    for g in range(key_heads):
        q = stage[:, (q_at + g) * LANES : (q_at + g + 1) * LANES]
        k = stage[:, (k_at + g) * LANES : (k_at + g + 1) * LANES]
        q = q * (lax.rsqrt(jnp.sum(q * q, axis=1, keepdims=True) + 1e-06) / math.sqrt(LANES))
        k = k * lax.rsqrt(jnp.sum(k * k, axis=1, keepdims=True) + 1e-06)
        qk = jnp.sum(q * k, axis=1, keepdims=True)
        k_hi = k.astype(BF16).astype(F32)
        q_hi = q.astype(BF16).astype(F32)
        lhs = jnp.concatenate([k_hi, k - k_hi, q_hi, q - q_hi], axis=0).astype(BF16)
        from_k = jnp.zeros((PAD, 2 * LANES), F32)
        from_q = jnp.zeros((PAD, 2 * LANES), F32)
        for r in range(count):
            row = arrival[r]
            both = jnp.concatenate([state[row, 2 * g], state[row, 2 * g + 1]], axis=1)
            got = mm(lhs, both)
            from_k = jnp.where(row8 == r, got[0:8] + got[8:16], from_k)
            from_q = jnp.where(row8 == r, got[16:24] + got[24:32], from_q)
        pair = []
        for i in range(2):
            h = 2 * g + i
            s = carry[:, h : h + 1]
            v = stage[:, (v_at + h) * LANES : (v_at + h + 1) * LANES]
            z = stage[:, (g_at + h) * LANES : (g_at + h + 1) * LANES]
            delta = beta[:, h : h + 1] * (v - s * from_k[:, i * LANES : (i + 1) * LANES])
            o = s * from_q[:, i * LANES : (i + 1) * LANES] + qk * delta
            norm = lax.rsqrt(jnp.mean(o * o, axis=1, keepdims=True) + 1e-06)
            pair.append(o * norm * gain * silu(z))
        g_pad[g * 16 : (g + 1) * 16, :] = jnp.concatenate(pair, axis=0).astype(BF16)
    row = iota((count * heads, heads * PAD), 0)
    col = iota((count * heads, heads * PAD), 1)
    filled = jnp.bitwise_and(col, 7) < count
    pack = (row == jnp.right_shift(col, 3) * count + jnp.bitwise_and(col, 7)) & filled
    g_src[...] = mm(pack.astype(BF16), g_pad[...]).astype(BF16)
    for y in ys:
        for c in (my_c, other):
            send(g_src, g_in.at[my_c * ny + my_y], 2, place_of(my_x, y, my_z, c))
    send(g_src, g_in.at[my_c * ny + my_y], 2, sibling)
    g_in[my_c * ny + my_y] = g_src[...]

    small[0, 0:count, 0:top] = (route_ids[...] + 1).astype(F32)
    small[1, 0:count, 0:top] = route_weight[...]
    r0_src[...] = pltpu.roll(small[0], my_y * top, 1).astype(BF16)
    stage[0:count, r_at * LANES : r_at * LANES + width] = residual[...].astype(F32)
    for y in range(ny):
        at = (r_at + y * y_chunks) * LANES
        tiles = [stage[:, at + i * LANES : at + (i + 1) * LANES] for i in range(y_chunks)]
        b_src[y] = jnp.concatenate(tiles, axis=0).astype(BF16)
    for y in ys:
        send(r0_src, r0_in.at[my_y], 0, place_of(my_x, y, my_z, my_c))
        send(b_src.at[y], b_in.at[my_y], 16, place_of(my_x, y, my_z, my_c))
    r0_in[my_y] = r0_src[...]
    b_in[my_y] = b_src[my_y]

    w_loads = []
    for e in range(2):
        for n, ref in ((0, gate_hbm), (2, up_hbm)):
            w_loads.append(
                pltpu.make_async_copy(
                    ref.at[e], w_in.at[:, pl.ds((n + e) * LANES, LANES)], load_sem.at[2 + n + e]
                )
            )
    own_width = pl.ds(pl.multiple_of(my_x * x_width, x_width), x_width)
    w_loads.append(
        pltpu.make_async_copy(down_hbm.at[:, :, own_width], w_down.at[my_x], load_sem.at[6])
    )
    for load in w_loads:
        load.start()

    w_own.wait()
    whole_wait(w_out.at[pl.ds(0, (nz - 1) * 16), :], recv_sem.at[1])
    row = iota((4 * heads * PAD, 4 * heads * count), 0)
    col = iota((4 * heads * PAD, 4 * heads * count), 1)
    filled = jnp.bitwise_and(row, 7) < count
    from_source = jnp.bitwise_and(jnp.right_shift(row, 3), 3)
    from_head = jnp.right_shift(row, 5)
    unpack = filled & (
        col == (from_source * heads + from_head) * count + jnp.bitwise_and(row, 7)
    )
    unpack = unpack.astype(BF16)
    whole_wait(g_in.at[pl.ds(0, 2 * ny - 1)], recv_sem.at[2])
    for n in range(0, 2 * ny, 4):
        four = mm(unpack, g_in[n : n + 4].reshape(4 * heads * count, LANES))
        g_all[:, n * PAD : (n + 4) * PAD] = four.astype(BF16).reshape(heads, 4 * PAD, LANES)
    part = jnp.zeros((2 * ny * PAD, cols), F32)
    for g in range(key_heads):
        rows = jnp.concatenate([g_all[2 * g], g_all[2 * g + 1]], axis=1)
        part += mm(rows, w_out[:, 2 * g * LANES : 2 * (g + 1) * LANES], NT)
    p_src[...] = part.reshape(2, nx, ROWS, cols)
    for x in far_first:
        for c in (my_c, other):
            send(p_src.at[c, x], p_in.at[my_c * nx + my_x], 4, place_of(x, my_y, my_z, c))
    send(p_src.at[other, my_x], p_in.at[my_c * nx + my_x], 4, sibling)
    p_in[my_c * nx + my_x] = p_src[my_c, my_x]
    whole_wait(r0_in.at[pl.ds(0, ny - 1)], recv_sem.at[0])
    ids = jnp.sum(r0_in[...].astype(F32), axis=0)
    r1_src[...] = ids.astype(BF16)
    for zc in zcs:
        send(r1_src, r1_in.at[my_zc], 3, at_zc(zc))
    r1_in[my_zc] = r1_src[...]

    here = y_chunks * ROWS
    sel_row = iota((32, LANES), 0)
    pick = jnp.bitwise_and(sel_row, 15)
    source = SRC * my_x + jnp.right_shift(sel_row, 4)
    sel = ((iota((32, LANES), 1) == source * top + pick) & (pick < top)).astype(F32)
    spread = (iota((PAD, here), 0) == jnp.bitwise_and(iota((PAD, here), 1), 7)).astype(F32)
    of_source = jnp.bitwise_and(jnp.right_shift(iota((16, here), 1), 3), 1)
    wide = mm(mm(sel, ids, NT, EXACT), spread, precision=EXACT)
    owner = jnp.where(of_source == 0, wide[0:16], wide[16:32])
    owner = jnp.floor((owner - 1.0) * 0.5).astype(jnp.int32)
    owner_row = iota((owners, here), 0)
    hit = jnp.zeros((owners, here), F32)
    for j in range(top):
        hit = hit + jnp.where(owner_row == owner[j : j + 1, :], 1.0, 0.0)
    each = (iota((owners * 4, owners), 1) == jnp.right_shift(iota((owners * 4, owners), 0), 2))
    row = iota((owners * 4, here), 0)
    col = iota((owners * 4, here), 1)
    match = (jnp.bitwise_and(jnp.right_shift(row, 1), 1) == jnp.bitwise_and(jnp.right_shift(col, 3), 1)) & (
        jnp.bitwise_and(row, 1) == jnp.right_shift(col, 4)
    )
    place[...] = jnp.where(match, mm(each.astype(BF16), hit.astype(BF16)), 0.0).astype(BF16)

    own_ids = small[0]
    own_weight = small[1]
    lane = iota((PAD, LANES), 1)
    share = jnp.zeros((PAD, owners), F32)
    for j in range(top):
        named = jnp.floor((own_ids[:, j : j + 1] - 1.0) * 0.5).astype(jnp.int32)
        share = share + jnp.where(lane == named, own_weight[:, j : j + 1], 0.0)
    hi = share.astype(BF16).astype(F32)
    open_up = iota((owners, back), 0) == jnp.right_shift(iota((owners, back), 1), 2)
    both = mm(jnp.concatenate([hi, share - hi], axis=0).astype(BF16), open_up.astype(BF16))
    row = iota((x_chunks * PAD, back), 0)
    kept = jnp.right_shift(row, 3) == jnp.bitwise_and(iota((x_chunks * PAD, back), 1), 3)
    for n in range(2):
        tall = jnp.concatenate([both[n * PAD : (n + 1) * PAD]] * x_chunks, axis=0)
        weigh[n] = jnp.where(kept, tall, 0.0).astype(BF16)

    mix_row = iota((2 * cols, 2 * cols), 0)
    mix_col = iota((2 * cols, 2 * cols), 1)
    mix = (
        (mix_row // cols == jnp.bitwise_and(jnp.right_shift(mix_col, 4), 1))
        & (
            jnp.right_shift(jnp.bitwise_and(mix_row, cols - 1), 4)
            == jnp.right_shift(mix_col, 5)
        )
        & (jnp.bitwise_and(mix_row, 15) == jnp.bitwise_and(mix_col, 15))
    )
    mix = mix.astype(BF16)

    whole_wait(b_in.at[pl.ds(0, ny - 1)], recv_sem.at[16])
    whole_wait(p_in.at[pl.ds(0, 2 * nx - 1)], recv_sem.at[4])
    attn = []
    for c in range(2):
        total = p_in[c * nx]
        for x in range(1, nx):
            total = total + p_in[c * nx + x]
        attn.append(total.astype(BF16))
    attn = mm(jnp.concatenate(attn, axis=1), mix)
    base_rows = [b_in[SRC * my_x + s].astype(F32) for s in range(SRC)]
    parts = []
    for i in range(y_chunks):
        base = jnp.concatenate([rows[i * PAD : (i + 1) * PAD] for rows in base_rows], axis=0)
        parts.append(base + attn[:, i * LANES : (i + 1) * LANES])
    carried = jnp.concatenate(parts, axis=0).astype(BF16)

    m3_src[...] = mm(place[...], carried).astype(BF16).reshape(owners, 4, LANES)
    for i, z in enumerate(z_to):
        for c in (my_c, other):
            for dy in Y_ORDER:
                y = lax.rem(my_y + dy, ny)
                to = place_of(my_x, y, z, c)
                src = m3_src.at[to[0]]
                dst = m3_in.at[i * 2 + my_c, my_y]
                if order[i] or dy or c is other:
                    send(src, dst, 20 + i // GROUP_Z, to)
                else:
                    pltpu.make_async_copy(src, dst, recv_sem.at[20 + i // GROUP_Z]).start()

    half = my_y - SRC * my_x
    wide = carried.astype(F32)
    to_x = my_y // SRC
    k_dst = k_in.at[my_y - SRC * to_x]
    k_copies = []
    for n in range(SRC):
        rows = [wide[i * ROWS + n * PAD : i * ROWS + (n + 1) * PAD] for i in range(y_chunks)]
        k_src[n] = jnp.concatenate(rows, axis=0).astype(BF16)
        away = remote(k_src.at[n], k_dst, 14, place_of(to_x, SRC * my_x + n, my_z, my_c))
        keep = pltpu.make_async_copy(k_src.at[n], k_dst, recv_sem.at[14])
        k_copies.append(away)

        @pl.when(half == n)
        def _():
            keep.start()

        @pl.when(half != n)
        def _():
            away.start()

    send(down_hbm.at[1, :, far_span], w_down.at[my_x, 1], 15, far)

    whole_wait(r1_in.at[pl.ds(0, nzc - 1)], recv_sem.at[3])
    slot = iota((groups * block, nzc), 0)
    slot_i = (slot // block) * GROUP_Z + jnp.bitwise_and(
        jnp.right_shift(slot, 2), GROUP_Z - 1
    )
    slot_z = jnp.zeros_like(slot)
    for i, z in enumerate(z_from):
        slot_z = jnp.where(slot_i == i, z, slot_z)
    slot_zc = slot_z * 2 + jnp.bitwise_and(jnp.right_shift(slot, 1), 1)
    of_zc = (slot_zc == iota((groups * block, nzc), 1)).astype(BF16)
    slot = iota((groups * block, LANES), 0)
    slot_x = jnp.bitwise_and(slot, block - 1) // per_x
    slot_y = SRC * slot_x + jnp.bitwise_and(slot, 1)
    lane = iota((groups * block, LANES), 1)
    of_y = (lane >= slot_y * top) & (lane < slot_y * top + top)
    arrived = r1_in[...].astype(F32)
    for e in range(2):
        named = (2 * ep + 1 + e).astype(F32)
        found = jnp.sum(jnp.where(arrived == named, 1.0, 0.0), axis=1).astype(BF16)
        found = jnp.where(of_y, mm(of_zc, found), 0.0)
        masks[e] = jnp.broadcast_to(
            jnp.sum(found, axis=1, keepdims=True), (groups * block, LANES)
        )

    turn_row = iota((flat, flat), 0)
    turn_col = iota((flat, flat), 1)
    turn_ch = turn_row // per_x
    turn_slot = turn_row % per_x
    unflat = turn_col == (
        (turn_slot // 2) * (ny * 4)
        + (turn_ch // y_chunks) * 4
        + jnp.bitwise_and(turn_slot, 1) * y_chunks
        + turn_ch % y_chunks
    )
    unflat = unflat.astype(BF16)
    for n in GROUP_ORDER:
        whole_wait(m3_in.at[pl.ds(n * g_zc, g_zc)], recv_sem.at[20 + n])
        turned = mm(unflat, m3_in[n * g_zc : (n + 1) * g_zc].reshape(flat, LANES))
        squares = jnp.zeros((per_x, LANES), F32)
        for ch in range(chunks):
            c = turned[ch * per_x : (ch + 1) * per_x]
            squares = squares + c * c
        norm = lax.rsqrt(jnp.sum(squares, axis=1, keepdims=True) / width + 1e-06)
        for ch in range(chunks):
            c = turned[ch * per_x : (ch + 1) * per_x]
            span = slice(ch * LANES, (ch + 1) * LANES)
            x_src[n, :, span] = (c * norm * ffn_gain[:, span]).astype(BF16)
        for x in near_first:
            send(x_src.at[n], x_in.at[n, my_x], 24 + n, place_of(x, my_y, my_z, my_c))
        x_in[n, my_x] = x_src[n]

    back_row = iota((block * x_chunks, block * x_chunks), 0)
    back_col = iota((block * x_chunks, block * x_chunks), 1)
    each_zc = ny * x_chunks
    row_y = (back_row % each_zc) // x_chunks
    slot = back_col % per_x
    flatten = (
        (back_row // each_zc == jnp.right_shift(slot, 1))
        & (row_y == SRC * (back_col // (per_x * x_chunks)) + jnp.bitwise_and(slot, 1))
        & (back_row % x_chunks == (back_col // per_x) % x_chunks)
    )
    flatten = flatten.astype(BF16)
    for load in w_loads:
        load.wait()

    def hidden_of(n):
        whole_wait(x_in.at[n, pl.ds(0, nx - 1)], recv_sem.at[24 + n])
        both = mm(x_in[n].reshape(block, width), w_in[...])
        hidden = jnp.zeros((block, LANES), F32)
        for e in range(2):
            gate = both[:, e * LANES : (e + 1) * LANES]
            up = both[:, (2 + e) * LANES : (3 + e) * LANES]
            hidden = hidden + silu(gate) * up * masks[e, n * block : (n + 1) * block]
        h_src[n] = hidden.astype(BF16)
        for x in far_first:
            send(h_src.at[n], h_in.at[n, my_x], 28 + n, place_of(x, my_y, my_z, my_c))
        h_in[n, my_x] = h_src[n]

    def output_of(n):
        whole_wait(h_in.at[n, pl.ds(0, nx - 1)], recv_sem.at[28 + n])
        parts = []
        for x in range(nx):
            h = h_in[n, x].astype(F32)
            for e in range(2):
                parts.append(h * masks[e, n * block : (n + 1) * block])
        total = mm(
            jnp.concatenate(parts, axis=1).astype(BF16),
            w_down[...].reshape(nx * 2 * LANES, x_width),
        )
        tiles = [
            total[x * per_x : (x + 1) * per_x, ch * LANES : (ch + 1) * LANES]
            for x in range(nx)
            for ch in range(x_chunks)
        ]
        turned = mm(flatten, jnp.concatenate(tiles, axis=0).astype(BF16)).astype(BF16)
        m6_src[n * g_zc : (n + 1) * g_zc] = turned.reshape(g_zc, ny, 4, LANES)
        for i in range(n * GROUP_Z, (n + 1) * GROUP_Z):
            for c in (my_c, other):
                for dy in Y_ORDER:
                    y = lax.rem(my_y + dy, ny)
                    src = m6_src.at[i * 2 + c, y]
                    if order[i] or dy or c is other:
                        send(src, m6_in.at[ep], 12, place_of(my_x, y, z_from[i], c))
                    else:
                        m6_in[ep] = m6_src[i * 2 + my_c, my_y]

    lag = groups
    for k, n in enumerate(GROUP_ORDER):
        hidden_of(n)
        if k == lag - 1:
            whole_wait(w_down.at[pl.ds(0, nx - 1)], recv_sem.at[15])
        if k >= lag:
            output_of(GROUP_ORDER[k - lag])
    for n in GROUP_ORDER[groups - lag :]:
        output_of(n)

    whole_wait(k_in, recv_sem.at[14])
    whole_wait(m6_in.at[pl.ds(0, owners - 1)], recv_sem.at[12])
    rows = m6_in[...].reshape(back, LANES)
    mixed = mm(weigh[0], rows) + mm(weigh[1], rows)
    mixed = mixed + k_in[...].reshape(x_chunks * PAD, LANES).astype(F32)
    for i in range(x_chunks):
        out[:, i * LANES : (i + 1) * LANES] = mixed[i * PAD : i * PAD + count].astype(BF16)

    for copy in sent:
        copy.wait_send()
    for n, copy in enumerate(k_copies):

        @pl.when(half != n)
        def _():
            copy.wait_send()


def shards(
    nx,
    ny,
    nzc,
    residual_in,
    new_query,
    new_keys,
    new_values,
    out_gate,
    beta_logit,
    decay_logit,
    decay_base,
    decay_bias,
    norm_gain,
    state_store,
    state_scale,
    arrival,
    out_weight,
    ffn_gain,
    expert_gate_weight,
    expert_up_weight,
    expert_down_weight,
    route_ids,
    route_weight,
):
    count, width = residual_in.shape
    key_heads = new_query.shape[1] // LANES
    heads = 2 * key_heads
    top = route_ids.shape[1]
    chunks = width // LANES
    y_chunks = chunks // ny
    x_chunks = chunks // nx
    owners = ny * nzc
    cols = nzc // 2 * 16
    groups = nzc // 2 // GROUP_Z
    per_x = GROUP_Z * 2 * SRC
    block = nx * per_x
    stage_tiles = 2 * key_heads + 2 * heads + chunks
    vmem = pl.BlockSpec(memory_space=pltpu.VMEM)
    hbm = pl.BlockSpec(memory_space=pltpu.HBM)
    small_operands = (
        residual_in,
        new_query,
        new_keys,
        new_values,
        out_gate,
        beta_logit,
        decay_logit,
        decay_base[None, :],
        decay_bias[None, :],
        norm_gain[None, :],
        state_scale,
        arrival,
        ffn_gain[None, :],
        route_ids,
        route_weight,
    )
    scratch = [
        (pltpu.SMEM if a is arrival else pltpu.VMEM)(a.shape, a.dtype) for a in small_operands
    ] + [
        pltpu.VMEM((PAD, stage_tiles * LANES), F32),
        pltpu.VMEM((4, PAD, LANES), F32),
        pltpu.VMEM(state_store.shape, BF16),
        pltpu.VMEM((width, 4 * LANES), BF16),
        pltpu.VMEM((nx, 2, LANES, width // nx), BF16),
        pltpu.VMEM((cols, heads * LANES), BF16),
        pltpu.VMEM((PAD, LANES), BF16),
        pltpu.VMEM((ny, PAD, LANES), BF16),
        pltpu.VMEM((ny, y_chunks * PAD, LANES), BF16),
        pltpu.VMEM((ny, y_chunks * PAD, LANES), BF16),
        pltpu.VMEM((PAD, LANES), BF16),
        pltpu.VMEM((nzc, PAD, LANES), BF16),
        pltpu.VMEM((heads * PAD, LANES), BF16),
        pltpu.VMEM((heads * count, LANES), BF16),
        pltpu.VMEM((2 * ny, heads * count, LANES), BF16),
        pltpu.VMEM((heads, 2 * ny * PAD, LANES), BF16),
        pltpu.VMEM((2, nx, ROWS, cols), F32),
        pltpu.VMEM((2 * nx, ROWS, cols), F32),
        pltpu.VMEM((SRC, y_chunks * PAD, LANES), BF16),
        pltpu.VMEM((SRC, y_chunks * PAD, LANES), BF16),
        pltpu.VMEM((owners * 4, y_chunks * ROWS), BF16),
        pltpu.VMEM((2, x_chunks * PAD, owners * 4), BF16),
        pltpu.VMEM((2, groups * block, LANES), F32),
        pltpu.VMEM((owners, 4, LANES), BF16),
        pltpu.VMEM((nzc, ny, 4, LANES), BF16),
        pltpu.VMEM((groups, per_x, width), BF16),
        pltpu.VMEM((groups, nx, per_x, width), BF16),
        pltpu.VMEM((groups, block, LANES), BF16),
        pltpu.VMEM((groups, nx, block, LANES), BF16),
        pltpu.VMEM((nzc, ny, 4, LANES), BF16),
        pltpu.VMEM((owners, 4, LANES), BF16),
        pltpu.SemaphoreType.DMA((len(small_operands),)),
        pltpu.SemaphoreType.DMA((8,)),
        pltpu.SemaphoreType.DMA((32,)),
        pltpu.SemaphoreType.DMA((32,)),
    ]
    return pl.pallas_call(
        functools.partial(kernel, nx, ny, nzc, top),
        out_shape=pltpu.VMEM((count, width // nx), BF16),
        in_specs=[hbm] * (len(small_operands) + 5),
        out_specs=vmem,
        scratch_shapes=scratch,
        compiler_params=pltpu.CompilerParams(
            collective_id=0, has_side_effects=True, vmem_limit_bytes=60 * 1024 * 1024
        ),
        name="decode_layer",
    )(
        *small_operands,
        out_weight.T,
        state_store,
        expert_gate_weight,
        expert_up_weight,
        expert_down_weight,
    )


def solution(mesh):
    nx = mesh.shape["tp"]
    ny = SRC * nx
    nzc = mesh.shape["ep"] // ny
    return jax.shard_map(
        functools.partial(shards, nx, ny, nzc),
        mesh=mesh,
        in_specs=(
            P("ep", None),
            P("ep", "tp"),
            P("ep", "tp"),
            P("ep", "tp"),
            P("ep", "tp"),
            P("ep", "tp"),
            P("ep", "tp"),
            P("tp"),
            P("tp"),
            P(),
            P("ep", "tp", None, None),
            P("ep", "tp"),
            P("ep"),
            P("tp", "ep"),
            P(),
            P("ep", None, "tp"),
            P("ep", None, "tp"),
            P("ep", "tp", None),
            P("ep", None),
            P("ep", None),
        ),
        out_specs=P("ep", "tp"),
        check_vma=False,
    )
```

```python
import functools
import math

import jax
import jax.numpy as jnp
from jax import lax
from jax.experimental import pallas as pl
from jax.experimental.pallas import tpu as pltpu
from jax.sharding import PartitionSpec as P

MESH = pl.DeviceIdType.MESH
F32 = jnp.float32
BF16 = jnp.bfloat16
LANES = 128
PAD = 8
SRC = 2
Z_ORDER = (0, 1, 7, 2, 6, 3, 5, 4)
GROUP_Z = 2
GROUP_ORDER = (0, 1, 2, 3)
Y_ORDER = (4, 3, 5, 2, 6, 1, 7, 0)
ROWS = SRC * PAD
NT = (((1,), (1,)), ((), ()))
EXACT = lax.Precision.HIGHEST


def mm(a, b, dims=(((1,), (0,)), ((), ())), precision=None):
    return lax.dot_general(a, b, dims, preferred_element_type=F32, precision=precision)


def iota(shape, axis):
    return lax.broadcasted_iota(jnp.int32, shape, axis)


def silu(v):
    return v * jax.nn.sigmoid(v)


def whole_wait(ref, sem):
    pltpu.make_async_copy(ref, ref, sem).wait()


def kernel(
    nx,
    ny,
    nzc,
    top,
    residual_hbm,
    query_hbm,
    keys_hbm,
    values_hbm,
    out_gate_hbm,
    beta_logit_hbm,
    decay_logit_hbm,
    decay_base_hbm,
    decay_bias_hbm,
    norm_gain_hbm,
    state_scale_hbm,
    arrival_hbm,
    ffn_gain_hbm,
    route_ids_hbm,
    route_weight_hbm,
    out_weight_hbm,
    state_hbm,
    gate_hbm,
    up_hbm,
    down_hbm,
    out,
    residual,
    query,
    keys,
    values,
    out_gate,
    beta_logit,
    decay_logit,
    decay_base,
    decay_bias,
    norm_gain,
    state_scale,
    arrival,
    ffn_gain,
    route_ids,
    route_weight,
    stage,
    small,
    state,
    w_in,
    w_down,
    w_out,
    r0_src,
    r0_in,
    b_src,
    b_in,
    r1_src,
    r1_in,
    g_pad,
    g_src,
    g_in,
    g_all,
    p_src,
    p_in,
    k_src,
    k_in,
    place,
    weigh,
    masks,
    m3_src,
    m3_in,
    x_src,
    x_in,
    h_src,
    h_in,
    m6_src,
    m6_in,
    small_sem,
    load_sem,
    send_sem,
    recv_sem,
):
    count, width = residual_hbm.shape
    chunks = width // LANES
    y_chunks = chunks // ny
    x_chunks = chunks // nx
    key_heads = query_hbm.shape[1] // LANES
    heads = 2 * key_heads
    nz = nzc // 2
    cols = nz * 16
    per_x = GROUP_Z * 2 * SRC
    flat = per_x * chunks
    owners = ny * nzc
    back = owners * 4
    groups = nz // GROUP_Z
    g_zc = 2 * GROUP_Z
    block = nx * per_x

    ep = lax.axis_index("ep")
    my_x = lax.axis_index("tp")
    my_y = ep // nzc
    my_zc = lax.rem(ep, nzc)
    my_z = my_zc // 2
    my_c = lax.rem(my_zc, 2)
    other = 1 - my_c

    def place_of(x, y, z, c):
        return (y * nzc + z * 2 + c, x)

    def at_zc(zc):
        return (my_y * nzc + zc, my_x)

    xs = [lax.rem(my_x + d, nx) for d in range(1, nx)]
    near_first = xs[0:1] + xs[2:] + xs[1:2]
    far_first = xs[1:2] + xs[0:1] + xs[2:]
    ys = [lax.rem(my_y + d, ny) for d in Y_ORDER if d]
    zs = [lax.rem(my_z + d, nz) for d in Y_ORDER if d]
    zcs = [lax.rem(my_zc + d, nzc) for d in range(1, nzc)]
    sibling = place_of(my_x, my_y, my_z, other)

    order = Z_ORDER
    z_from = [lax.rem(my_z + d, nz) for d in order]
    z_to = [lax.rem(my_z + nz - d, nz) for d in order]

    sent = []

    def remote(src, dst, hop, target):
        return pltpu.make_async_remote_copy(
            src_ref=src,
            dst_ref=dst,
            send_sem=send_sem.at[hop],
            recv_sem=recv_sem.at[hop],
            device_id=target,
            device_id_type=MESH,
        )

    def send(src, dst, hop, target):
        copy = remote(src, dst, hop, target)
        copy.start()
        sent.append(copy)

    own_cols = pl.ds(pl.multiple_of(my_z * 16, 16), 16)
    smalls = [
        pltpu.make_async_copy(src, dst, small_sem.at[n])
        for n, (src, dst) in enumerate(
            (
                (route_ids_hbm, route_ids),
                (route_weight_hbm, route_weight),
                (residual_hbm, residual),
                (query_hbm, query),
                (keys_hbm, keys),
                (values_hbm, values),
                (out_gate_hbm, out_gate),
                (beta_logit_hbm, beta_logit),
                (decay_logit_hbm, decay_logit),
                (decay_base_hbm, decay_base),
                (decay_bias_hbm, decay_bias),
                (norm_gain_hbm, norm_gain),
                (state_scale_hbm, state_scale),
                (arrival_hbm, arrival),
                (ffn_gain_hbm, ffn_gain),
            )
        )
    ]
    for load in smalls:
        load.start()
    state_load = pltpu.make_async_copy(state_hbm, state, load_sem.at[0])
    state_load.start()
    w_own = pltpu.make_async_copy(out_weight_hbm, w_out.at[own_cols, :], load_sem.at[1])
    w_own.start()

    barrier = pltpu.get_barrier_semaphore()
    peers = [
        place_of(my_x, lax.rem(my_y + d, ny), my_z, c) for d in Y_ORDER for c in (my_c, other) if d
    ]
    peers += [place_of(my_x, my_y, lax.rem(my_z + d, nz), my_c) for d in Y_ORDER if d]
    peers += [place_of(x, my_y, my_z, my_c) for x in xs]
    peers.append(sibling)
    for peer in peers:
        pl.semaphore_signal(barrier, inc=1, device_id=peer, device_id_type=MESH)
    pl.semaphore_wait(barrier, len(peers))

    for z in zs:
        send(out_weight_hbm, w_out.at[own_cols, :], 1, place_of(my_x, my_y, z, my_c))

    x_width = x_chunks * LANES
    for x in near_first[0:2]:
        span = pl.ds(pl.multiple_of(x * x_width, x_width), x_width)
        send(down_hbm.at[:, :, span], w_down.at[my_x], 15, place_of(x, my_y, my_z, my_c))
    far = place_of(xs[1], my_y, my_z, my_c)
    far_span = pl.ds(pl.multiple_of(xs[1] * x_width, x_width), x_width)
    send(down_hbm.at[0, :, far_span], w_down.at[my_x, 0], 15, far)

    stage[...] = jnp.zeros_like(stage)
    small[...] = jnp.zeros_like(small)
    q_at, k_at, v_at, g_at = 0, key_heads, 2 * key_heads, 2 * key_heads + heads
    r_at = g_at + heads
    for load in smalls:
        load.wait()
    for at, ref in ((q_at, query), (k_at, keys), (v_at, values), (g_at, out_gate)):
        stage[0:count, at * LANES : at * LANES + ref.shape[1]] = ref[...].astype(F32)
    small[2, 0:count, 0:heads] = decay_logit[...]
    small[3, 0:count, 0:heads] = beta_logit[...]
    rate = jnp.exp(decay_base[...])
    logit = small[2, :, 0:heads] + decay_bias[...]
    soft = jnp.maximum(logit, 0.0) + jnp.log1p(jnp.exp(-jnp.abs(logit)))
    decay = jnp.exp(-rate * soft)
    beta = jax.nn.sigmoid(small[3, :, 0:heads])
    row8 = iota((PAD, 1), 0)
    moved = jnp.zeros((PAD, heads), F32)
    for r in range(count):
        moved = jnp.where(row8 == r, state_scale[pl.ds(arrival[r], 1), :], moved)
    carry = moved * decay
    gain = norm_gain[...]
    state_load.wait()
    for g in range(key_heads):
        q = stage[:, (q_at + g) * LANES : (q_at + g + 1) * LANES]
        k = stage[:, (k_at + g) * LANES : (k_at + g + 1) * LANES]
        q = q * (lax.rsqrt(jnp.sum(q * q, axis=1, keepdims=True) + 1e-06) / math.sqrt(LANES))
        k = k * lax.rsqrt(jnp.sum(k * k, axis=1, keepdims=True) + 1e-06)
        qk = jnp.sum(q * k, axis=1, keepdims=True)
        k_hi = k.astype(BF16).astype(F32)
        q_hi = q.astype(BF16).astype(F32)
        lhs = jnp.concatenate([k_hi, k - k_hi, q_hi, q - q_hi], axis=0).astype(BF16)
        from_k = jnp.zeros((PAD, 2 * LANES), F32)
        from_q = jnp.zeros((PAD, 2 * LANES), F32)
        for r in range(count):
            row = arrival[r]
            both = jnp.concatenate([state[row, 2 * g], state[row, 2 * g + 1]], axis=1)
            got = mm(lhs, both)
            from_k = jnp.where(row8 == r, got[0:8] + got[8:16], from_k)
            from_q = jnp.where(row8 == r, got[16:24] + got[24:32], from_q)
        pair = []
        for i in range(2):
            h = 2 * g + i
            s = carry[:, h : h + 1]
            v = stage[:, (v_at + h) * LANES : (v_at + h + 1) * LANES]
            z = stage[:, (g_at + h) * LANES : (g_at + h + 1) * LANES]
            delta = beta[:, h : h + 1] * (v - s * from_k[:, i * LANES : (i + 1) * LANES])
            o = s * from_q[:, i * LANES : (i + 1) * LANES] + qk * delta
            norm = lax.rsqrt(jnp.mean(o * o, axis=1, keepdims=True) + 1e-06)
            pair.append(o * norm * gain * silu(z))
        g_pad[g * 16 : (g + 1) * 16, :] = jnp.concatenate(pair, axis=0).astype(BF16)
    row = iota((count * heads, heads * PAD), 0)
    col = iota((count * heads, heads * PAD), 1)
    filled = jnp.bitwise_and(col, 7) < count
    pack = (row == jnp.right_shift(col, 3) * count + jnp.bitwise_and(col, 7)) & filled
    g_src[...] = mm(pack.astype(BF16), g_pad[...]).astype(BF16)
    for y in ys:
        for c in (my_c, other):
            send(g_src, g_in.at[my_c * ny + my_y], 2, place_of(my_x, y, my_z, c))
    send(g_src, g_in.at[my_c * ny + my_y], 2, sibling)
    g_in[my_c * ny + my_y] = g_src[...]

    small[0, 0:count, 0:top] = (route_ids[...] + 1).astype(F32)
    small[1, 0:count, 0:top] = route_weight[...]
    r0_src[...] = pltpu.roll(small[0], my_y * top, 1).astype(BF16)
    stage[0:count, r_at * LANES : r_at * LANES + width] = residual[...].astype(F32)
    for y in range(ny):
        at = (r_at + y * y_chunks) * LANES
        tiles = [stage[:, at + i * LANES : at + (i + 1) * LANES] for i in range(y_chunks)]
        b_src[y] = jnp.concatenate(tiles, axis=0).astype(BF16)
    for y in ys:
        send(r0_src, r0_in.at[my_y], 0, place_of(my_x, y, my_z, my_c))
        send(b_src.at[y], b_in.at[my_y], 16, place_of(my_x, y, my_z, my_c))
    r0_in[my_y] = r0_src[...]
    b_in[my_y] = b_src[my_y]

    w_loads = []
    for e in range(2):
        for n, ref in ((0, gate_hbm), (2, up_hbm)):
            w_loads.append(
                pltpu.make_async_copy(
                    ref.at[e], w_in.at[:, pl.ds((n + e) * LANES, LANES)], load_sem.at[2 + n + e]
                )
            )
    own_width = pl.ds(pl.multiple_of(my_x * x_width, x_width), x_width)
    w_loads.append(
        pltpu.make_async_copy(down_hbm.at[:, :, own_width], w_down.at[my_x], load_sem.at[6])
    )
    for load in w_loads:
        load.start()

    w_own.wait()
    whole_wait(w_out.at[pl.ds(0, (nz - 1) * 16), :], recv_sem.at[1])
    row = iota((4 * heads * PAD, 4 * heads * count), 0)
    col = iota((4 * heads * PAD, 4 * heads * count), 1)
    filled = jnp.bitwise_and(row, 7) < count
    from_source = jnp.bitwise_and(jnp.right_shift(row, 3), 3)
    from_head = jnp.right_shift(row, 5)
    unpack = filled & (
        col == (from_source * heads + from_head) * count + jnp.bitwise_and(row, 7)
    )
    unpack = unpack.astype(BF16)
    whole_wait(g_in.at[pl.ds(0, 2 * ny - 1)], recv_sem.at[2])
    for n in range(0, 2 * ny, 4):
        four = mm(unpack, g_in[n : n + 4].reshape(4 * heads * count, LANES))
        g_all[:, n * PAD : (n + 4) * PAD] = four.astype(BF16).reshape(heads, 4 * PAD, LANES)
    part = jnp.zeros((2 * ny * PAD, cols), F32)
    for g in range(key_heads):
        rows = jnp.concatenate([g_all[2 * g], g_all[2 * g + 1]], axis=1)
        part += mm(rows, w_out[:, 2 * g * LANES : 2 * (g + 1) * LANES], NT)
    p_src[...] = part.reshape(2, nx, ROWS, cols)
    for x in far_first:
        for c in (my_c, other):
            send(p_src.at[c, x], p_in.at[my_c * nx + my_x], 4, place_of(x, my_y, my_z, c))
    send(p_src.at[other, my_x], p_in.at[my_c * nx + my_x], 4, sibling)
    p_in[my_c * nx + my_x] = p_src[my_c, my_x]
    whole_wait(r0_in.at[pl.ds(0, ny - 1)], recv_sem.at[0])
    ids = jnp.sum(r0_in[...].astype(F32), axis=0)
    r1_src[...] = ids.astype(BF16)
    for zc in zcs:
        send(r1_src, r1_in.at[my_zc], 3, at_zc(zc))
    r1_in[my_zc] = r1_src[...]

    here = y_chunks * ROWS
    sel_row = iota((32, LANES), 0)
    pick = jnp.bitwise_and(sel_row, 15)
    source = SRC * my_x + jnp.right_shift(sel_row, 4)
    sel = ((iota((32, LANES), 1) == source * top + pick) & (pick < top)).astype(F32)
    spread = (iota((PAD, here), 0) == jnp.bitwise_and(iota((PAD, here), 1), 7)).astype(F32)
    of_source = jnp.bitwise_and(jnp.right_shift(iota((16, here), 1), 3), 1)
    wide = mm(mm(sel, ids, NT, EXACT), spread, precision=EXACT)
    owner = jnp.where(of_source == 0, wide[0:16], wide[16:32])
    owner = jnp.floor((owner - 1.0) * 0.5).astype(jnp.int32)
    owner_row = iota((owners, here), 0)
    hit = jnp.zeros((owners, here), F32)
    for j in range(top):
        hit = hit + jnp.where(owner_row == owner[j : j + 1, :], 1.0, 0.0)
    each = (iota((owners * 4, owners), 1) == jnp.right_shift(iota((owners * 4, owners), 0), 2))
    row = iota((owners * 4, here), 0)
    col = iota((owners * 4, here), 1)
    match = (jnp.bitwise_and(jnp.right_shift(row, 1), 1) == jnp.bitwise_and(jnp.right_shift(col, 3), 1)) & (
        jnp.bitwise_and(row, 1) == jnp.right_shift(col, 4)
    )
    place[...] = jnp.where(match, mm(each.astype(BF16), hit.astype(BF16)), 0.0).astype(BF16)

    own_ids = small[0]
    own_weight = small[1]
    lane = iota((PAD, LANES), 1)
    share = jnp.zeros((PAD, owners), F32)
    for j in range(top):
        named = jnp.floor((own_ids[:, j : j + 1] - 1.0) * 0.5).astype(jnp.int32)
        share = share + jnp.where(lane == named, own_weight[:, j : j + 1], 0.0)
    hi = share.astype(BF16).astype(F32)
    open_up = iota((owners, back), 0) == jnp.right_shift(iota((owners, back), 1), 2)
    both = mm(jnp.concatenate([hi, share - hi], axis=0).astype(BF16), open_up.astype(BF16))
    row = iota((x_chunks * PAD, back), 0)
    kept = jnp.right_shift(row, 3) == jnp.bitwise_and(iota((x_chunks * PAD, back), 1), 3)
    for n in range(2):
        tall = jnp.concatenate([both[n * PAD : (n + 1) * PAD]] * x_chunks, axis=0)
        weigh[n] = jnp.where(kept, tall, 0.0).astype(BF16)

    mix_row = iota((2 * cols, 2 * cols), 0)
    mix_col = iota((2 * cols, 2 * cols), 1)
    mix = (
        (mix_row // cols == jnp.bitwise_and(jnp.right_shift(mix_col, 4), 1))
        & (
            jnp.right_shift(jnp.bitwise_and(mix_row, cols - 1), 4)
            == jnp.right_shift(mix_col, 5)
        )
        & (jnp.bitwise_and(mix_row, 15) == jnp.bitwise_and(mix_col, 15))
    )
    mix = mix.astype(BF16)

    whole_wait(b_in.at[pl.ds(0, ny - 1)], recv_sem.at[16])
    whole_wait(p_in.at[pl.ds(0, 2 * nx - 1)], recv_sem.at[4])
    attn = []
    for c in range(2):
        total = p_in[c * nx]
        for x in range(1, nx):
            total = total + p_in[c * nx + x]
        attn.append(total.astype(BF16))
    attn = mm(jnp.concatenate(attn, axis=1), mix)
    base_rows = [b_in[SRC * my_x + s].astype(F32) for s in range(SRC)]
    parts = []
    for i in range(y_chunks):
        base = jnp.concatenate([rows[i * PAD : (i + 1) * PAD] for rows in base_rows], axis=0)
        parts.append(base + attn[:, i * LANES : (i + 1) * LANES])
    carried = jnp.concatenate(parts, axis=0).astype(BF16)

    m3_src[...] = mm(place[...], carried).astype(BF16).reshape(owners, 4, LANES)
    for i, z in enumerate(z_to):
        for dy in Y_ORDER:
            for c in (other, my_c):
                y = lax.rem(my_y + dy, ny)
                to = place_of(my_x, y, z, c)
                src = m3_src.at[to[0]]
                dst = m3_in.at[i * 2 + my_c, my_y]
                if order[i] or dy or c is other:
                    send(src, dst, 20 + i // GROUP_Z, to)
                else:
                    pltpu.make_async_copy(src, dst, recv_sem.at[20 + i // GROUP_Z]).start()

    half = my_y - SRC * my_x
    wide = carried.astype(F32)
    to_x = my_y // SRC
    k_dst = k_in.at[my_y - SRC * to_x]
    k_copies = []
    for n in range(SRC):
        rows = [wide[i * ROWS + n * PAD : i * ROWS + (n + 1) * PAD] for i in range(y_chunks)]
        k_src[n] = jnp.concatenate(rows, axis=0).astype(BF16)
        away = remote(k_src.at[n], k_dst, 14, place_of(to_x, SRC * my_x + n, my_z, my_c))
        keep = pltpu.make_async_copy(k_src.at[n], k_dst, recv_sem.at[14])
        k_copies.append(away)

        @pl.when(half == n)
        def _():
            keep.start()

        @pl.when(half != n)
        def _():
            away.start()

    send(down_hbm.at[1, :, far_span], w_down.at[my_x, 1], 15, far)

    whole_wait(r1_in.at[pl.ds(0, nzc - 1)], recv_sem.at[3])
    slot = iota((groups * block, nzc), 0)
    slot_i = (slot // block) * GROUP_Z + jnp.bitwise_and(
        jnp.right_shift(slot, 2), GROUP_Z - 1
    )
    slot_z = jnp.zeros_like(slot)
    for i, z in enumerate(z_from):
        slot_z = jnp.where(slot_i == i, z, slot_z)
    slot_zc = slot_z * 2 + jnp.bitwise_and(jnp.right_shift(slot, 1), 1)
    of_zc = (slot_zc == iota((groups * block, nzc), 1)).astype(BF16)
    slot = iota((groups * block, LANES), 0)
    slot_x = jnp.bitwise_and(slot, block - 1) // per_x
    slot_y = SRC * slot_x + jnp.bitwise_and(slot, 1)
    lane = iota((groups * block, LANES), 1)
    of_y = (lane >= slot_y * top) & (lane < slot_y * top + top)
    arrived = r1_in[...].astype(F32)
    for e in range(2):
        named = (2 * ep + 1 + e).astype(F32)
        found = jnp.sum(jnp.where(arrived == named, 1.0, 0.0), axis=1).astype(BF16)
        found = jnp.where(of_y, mm(of_zc, found), 0.0)
        masks[e] = jnp.broadcast_to(
            jnp.sum(found, axis=1, keepdims=True), (groups * block, LANES)
        )

    turn_row = iota((flat, flat), 0)
    turn_col = iota((flat, flat), 1)
    turn_ch = turn_row // per_x
    turn_slot = turn_row % per_x
    unflat = turn_col == (
        (turn_slot // 2) * (ny * 4)
        + (turn_ch // y_chunks) * 4
        + jnp.bitwise_and(turn_slot, 1) * y_chunks
        + turn_ch % y_chunks
    )
    unflat = unflat.astype(BF16)
    for n in GROUP_ORDER:
        whole_wait(m3_in.at[pl.ds(n * g_zc, g_zc)], recv_sem.at[20 + n])
        turned = mm(unflat, m3_in[n * g_zc : (n + 1) * g_zc].reshape(flat, LANES))
        squares = jnp.zeros((per_x, LANES), F32)
        for ch in range(chunks):
            c = turned[ch * per_x : (ch + 1) * per_x]
            squares = squares + c * c
        norm = lax.rsqrt(jnp.sum(squares, axis=1, keepdims=True) / width + 1e-06)
        for ch in range(chunks):
            c = turned[ch * per_x : (ch + 1) * per_x]
            span = slice(ch * LANES, (ch + 1) * LANES)
            x_src[n, :, span] = (c * norm * ffn_gain[:, span]).astype(BF16)
        for x in near_first:
            send(x_src.at[n], x_in.at[n, my_x], 24 + n, place_of(x, my_y, my_z, my_c))
        x_in[n, my_x] = x_src[n]

    back_row = iota((block * x_chunks, block * x_chunks), 0)
    back_col = iota((block * x_chunks, block * x_chunks), 1)
    each_zc = ny * x_chunks
    row_y = (back_row % each_zc) // x_chunks
    slot = back_col % per_x
    flatten = (
        (back_row // each_zc == jnp.right_shift(slot, 1))
        & (row_y == SRC * (back_col // (per_x * x_chunks)) + jnp.bitwise_and(slot, 1))
        & (back_row % x_chunks == (back_col // per_x) % x_chunks)
    )
    flatten = flatten.astype(BF16)
    for load in w_loads:
        load.wait()

    def hidden_of(n):
        whole_wait(x_in.at[n, pl.ds(0, nx - 1)], recv_sem.at[24 + n])
        both = mm(x_in[n].reshape(block, width), w_in[...])
        hidden = jnp.zeros((block, LANES), F32)
        for e in range(2):
            gate = both[:, e * LANES : (e + 1) * LANES]
            up = both[:, (2 + e) * LANES : (3 + e) * LANES]
            hidden = hidden + silu(gate) * up * masks[e, n * block : (n + 1) * block]
        h_src[n] = hidden.astype(BF16)
        for x in far_first:
            send(h_src.at[n], h_in.at[n, my_x], 28 + n, place_of(x, my_y, my_z, my_c))
        h_in[n, my_x] = h_src[n]

    def output_of(n):
        whole_wait(h_in.at[n, pl.ds(0, nx - 1)], recv_sem.at[28 + n])
        parts = []
        for x in range(nx):
            h = h_in[n, x].astype(F32)
            for e in range(2):
                parts.append(h * masks[e, n * block : (n + 1) * block])
        total = mm(
            jnp.concatenate(parts, axis=1).astype(BF16),
            w_down[...].reshape(nx * 2 * LANES, x_width),
        )
        tiles = [
            total[x * per_x : (x + 1) * per_x, ch * LANES : (ch + 1) * LANES]
            for x in range(nx)
            for ch in range(x_chunks)
        ]
        turned = mm(flatten, jnp.concatenate(tiles, axis=0).astype(BF16)).astype(BF16)
        m6_src[n * g_zc : (n + 1) * g_zc] = turned.reshape(g_zc, ny, 4, LANES)
        for i in reversed(range(n * GROUP_Z, (n + 1) * GROUP_Z)):
            for dy in Y_ORDER:
                for c in (other, my_c):
                    y = lax.rem(my_y + dy, ny)
                    src = m6_src.at[i * 2 + c, y]
                    if order[i] or dy or c is other:
                        send(src, m6_in.at[ep], 12, place_of(my_x, y, z_from[i], c))
                    else:
                        m6_in[ep] = m6_src[i * 2 + my_c, my_y]

    lag = groups
    for k, n in enumerate(GROUP_ORDER):
        hidden_of(n)
        if k == lag - 1:
            whole_wait(w_down.at[pl.ds(0, nx - 1)], recv_sem.at[15])
        if k >= lag:
            output_of(GROUP_ORDER[k - lag])
    for n in GROUP_ORDER[groups - lag :]:
        output_of(n)

    whole_wait(k_in, recv_sem.at[14])
    whole_wait(m6_in.at[pl.ds(0, owners - 1)], recv_sem.at[12])
    rows = m6_in[...].reshape(back, LANES)
    mixed = mm(weigh[0], rows) + mm(weigh[1], rows)
    mixed = mixed + k_in[...].reshape(x_chunks * PAD, LANES).astype(F32)
    for i in range(x_chunks):
        out[:, i * LANES : (i + 1) * LANES] = mixed[i * PAD : i * PAD + count].astype(BF16)

    for copy in sent:
        copy.wait_send()
    for n, copy in enumerate(k_copies):

        @pl.when(half != n)
        def _():
            copy.wait_send()


def shards(
    nx,
    ny,
    nzc,
    residual_in,
    new_query,
    new_keys,
    new_values,
    out_gate,
    beta_logit,
    decay_logit,
    decay_base,
    decay_bias,
    norm_gain,
    state_store,
    state_scale,
    arrival,
    out_weight,
    ffn_gain,
    expert_gate_weight,
    expert_up_weight,
    expert_down_weight,
    route_ids,
    route_weight,
):
    count, width = residual_in.shape
    key_heads = new_query.shape[1] // LANES
    heads = 2 * key_heads
    top = route_ids.shape[1]
    chunks = width // LANES
    y_chunks = chunks // ny
    x_chunks = chunks // nx
    owners = ny * nzc
    cols = nzc // 2 * 16
    groups = nzc // 2 // GROUP_Z
    per_x = GROUP_Z * 2 * SRC
    block = nx * per_x
    stage_tiles = 2 * key_heads + 2 * heads + chunks
    vmem = pl.BlockSpec(memory_space=pltpu.VMEM)
    hbm = pl.BlockSpec(memory_space=pltpu.HBM)
    small_operands = (
        residual_in,
        new_query,
        new_keys,
        new_values,
        out_gate,
        beta_logit,
        decay_logit,
        decay_base[None, :],
        decay_bias[None, :],
        norm_gain[None, :],
        state_scale,
        arrival,
        ffn_gain[None, :],
        route_ids,
        route_weight,
    )
    scratch = [
        (pltpu.SMEM if a is arrival else pltpu.VMEM)(a.shape, a.dtype) for a in small_operands
    ] + [
        pltpu.VMEM((PAD, stage_tiles * LANES), F32),
        pltpu.VMEM((4, PAD, LANES), F32),
        pltpu.VMEM(state_store.shape, BF16),
        pltpu.VMEM((width, 4 * LANES), BF16),
        pltpu.VMEM((nx, 2, LANES, width // nx), BF16),
        pltpu.VMEM((cols, heads * LANES), BF16),
        pltpu.VMEM((PAD, LANES), BF16),
        pltpu.VMEM((ny, PAD, LANES), BF16),
        pltpu.VMEM((ny, y_chunks * PAD, LANES), BF16),
        pltpu.VMEM((ny, y_chunks * PAD, LANES), BF16),
        pltpu.VMEM((PAD, LANES), BF16),
        pltpu.VMEM((nzc, PAD, LANES), BF16),
        pltpu.VMEM((heads * PAD, LANES), BF16),
        pltpu.VMEM((heads * count, LANES), BF16),
        pltpu.VMEM((2 * ny, heads * count, LANES), BF16),
        pltpu.VMEM((heads, 2 * ny * PAD, LANES), BF16),
        pltpu.VMEM((2, nx, ROWS, cols), F32),
        pltpu.VMEM((2 * nx, ROWS, cols), F32),
        pltpu.VMEM((SRC, y_chunks * PAD, LANES), BF16),
        pltpu.VMEM((SRC, y_chunks * PAD, LANES), BF16),
        pltpu.VMEM((owners * 4, y_chunks * ROWS), BF16),
        pltpu.VMEM((2, x_chunks * PAD, owners * 4), BF16),
        pltpu.VMEM((2, groups * block, LANES), F32),
        pltpu.VMEM((owners, 4, LANES), BF16),
        pltpu.VMEM((nzc, ny, 4, LANES), BF16),
        pltpu.VMEM((groups, per_x, width), BF16),
        pltpu.VMEM((groups, nx, per_x, width), BF16),
        pltpu.VMEM((groups, block, LANES), BF16),
        pltpu.VMEM((groups, nx, block, LANES), BF16),
        pltpu.VMEM((nzc, ny, 4, LANES), BF16),
        pltpu.VMEM((owners, 4, LANES), BF16),
        pltpu.SemaphoreType.DMA((len(small_operands),)),
        pltpu.SemaphoreType.DMA((8,)),
        pltpu.SemaphoreType.DMA((32,)),
        pltpu.SemaphoreType.DMA((32,)),
    ]
    return pl.pallas_call(
        functools.partial(kernel, nx, ny, nzc, top),
        out_shape=pltpu.VMEM((count, width // nx), BF16),
        in_specs=[hbm] * (len(small_operands) + 5),
        out_specs=vmem,
        scratch_shapes=scratch,
        compiler_params=pltpu.CompilerParams(
            collective_id=0, has_side_effects=True, vmem_limit_bytes=60 * 1024 * 1024
        ),
        name="decode_layer",
    )(
        *small_operands,
        out_weight.T,
        state_store,
        expert_gate_weight,
        expert_up_weight,
        expert_down_weight,
    )


def solution(mesh):
    nx = mesh.shape["tp"]
    ny = SRC * nx
    nzc = mesh.shape["ep"] // ny
    return jax.shard_map(
        functools.partial(shards, nx, ny, nzc),
        mesh=mesh,
        in_specs=(
            P("ep", None),
            P("ep", "tp"),
            P("ep", "tp"),
            P("ep", "tp"),
            P("ep", "tp"),
            P("ep", "tp"),
            P("ep", "tp"),
            P("tp"),
            P("tp"),
            P(),
            P("ep", "tp", None, None),
            P("ep", "tp"),
            P("ep"),
            P("tp", "ep"),
            P(),
            P("ep", None, "tp"),
            P("ep", None, "tp"),
            P("ep", "tp", None),
            P("ep", None),
            P("ep", None),
        ),
        out_specs=P("ep", "tp"),
        check_vma=False,
    )
```
